128 devices in a mesh: gx: 16 (over x, z), gy: 8 (over y, core).
Axes of the slice: x: 4, y: 4, z: 4, core: 2. Of those that a mesh axis runs over, the one named last changes fastest.
Arguments:
- particle_data: float32 [5, 128, 128, 3072], P(None, ('gx', 'gy')), as said below
- particle_cells: int32 [2, 128, 128, 3072], P(None, ('gx', 'gy')), may hold values from 0 to 1023, as said below
- slot_counts: int32 [128, 128], P(('gx', 'gy')), may hold values from 0 to 3072, as said below
- fluid_velocity: float32 [3, 64, 128, 1024], P(None, None, 'gx', 'gy'), may hold values from -6 to 6
Outputs:
- pressure: float32 [64, 128, 1024], P(None, 'gx', 'gy')
- drag_force: float32 [3, 128, 128, 3072], P(None, ('gx', 'gy'))
The draws below stay inside these ranges and needn't reach their ends.
Inputs may be any that keep to these rules, and one draw needn't show every extreme that they name: `slot_counts`: holder h has live particles only in the fluid boxes whose length position differs from box h's by at most 2 and whose width position differs by at most 1; elsewhere its counts are 0. In those boxes its counts are at least 384 and vary with a density level of the fluid box, from one to four; one of those boxes is full to 3072. `particle_data`: volumes lie between 0.5 and 3, drag coefficients between 0.5 and 5; velocities are of order one. `particle_cells`: row 0 holds heights 0 to 63, row 1 columns 0 to 1023.
All inputs are finite; a program needn't handle non-finite values.
Results may differ from the reference program's by a relative error of at most 0.0001.
Values sent between devices are 32-bit elements; how exact they have to be, the bound alone decides.
No kernel may reach another device: no remote copies, remote signals or barrier semaphores. Data moves between devices by JAX's collectives and lax.ppermute only.
A program may use at most 192 MiB of HBM per device.

```python
import math
import jax
import jax.numpy as jnp
from jax import lax

CX = 8
CY = 128
NZ = 64
CAP = 3072
ITERS = 3
NDEV = 128
NX = 128
NY = 1024
N_GX = 16
N_GY = 8


def draw_particle_data(key, part):
    key = jax.random.fold_in(key, 11)
    subkeys = jax.random.split(key, 3)
    extent = (NDEV, NDEV, CAP)
    volume = jnp.exp(jax.random.uniform(subkeys[0], extent, jnp.float32, math.log(0.5), math.log(3.0)))
    coefficient = jnp.exp(jax.random.uniform(subkeys[1], extent, jnp.float32, math.log(0.5), math.log(5.0)))
    velocity_draw = jnp.clip(jax.random.normal(subkeys[2], (3,) + extent, jnp.float32), -4.0, 4.0)
    return jnp.concatenate([volume[None], coefficient[None], velocity_draw], axis=0)


def draw_particle_cells(key, part):
    key = jax.random.fold_in(key, 13)
    first, second = jax.random.split(key, 2)
    extent = (NDEV, NDEV, CAP)
    heights = jax.random.randint(first, extent, 0, NZ)
    columns = jax.random.randint(second, extent, 0, CX * CY)
    flat = lax.broadcasted_iota(jnp.int32, extent, 2) + lax.broadcasted_iota(jnp.int32, extent, 1) * CAP + lax.broadcasted_iota(jnp.int32, extent, 0) * (NDEV * CAP)
    heights = jnp.where(flat == CAP - 1, NZ - 1, heights)
    columns = jnp.where(flat == CAP - 2, CX * CY - 1, columns)
    return jnp.stack([heights, columns]).astype(jnp.int32)


def draw_slot_counts(key, part):
    key = jax.random.fold_in(key, 12)
    first, second, third, fourth = jax.random.split(key, 4)
    levels = jax.random.randint(first, (NDEV,), 1, 5)
    lowest = levels * CAP // 8
    highest = levels * CAP // 4
    spread_bits = jax.random.randint(second, (NDEV, NDEV), 0, 1 << 20)
    counts_drawn = lowest[None, :] + spread_bits % (highest - lowest + 1)[None, :]
    holder = lax.broadcasted_iota(jnp.int32, (NDEV, NDEV), 0)
    column = lax.broadcasted_iota(jnp.int32, (NDEV, NDEV), 1)
    holder_x = holder // N_GY
    holder_y = holder % N_GY
    box_x = column // N_GY
    box_y = column % N_GY
    nearby = (jnp.abs(box_x - holder_x) <= 2) & (jnp.abs(box_y - holder_y) <= 1)
    holder_ids = jnp.arange(NDEV, dtype=jnp.int32)
    offset_x = jax.random.randint(third, (NDEV,), -2, 3)
    offset_y = jax.random.randint(fourth, (NDEV,), -1, 2)
    full_x = jnp.clip(holder_ids // N_GY + offset_x, 0, N_GX - 1)
    full_y = jnp.clip(holder_ids % N_GY + offset_y, 0, N_GY - 1)
    fullest = full_x * N_GY + full_y
    counts_near = jnp.where(column == fullest[:, None], CAP, counts_drawn)
    return jnp.where(nearby, counts_near, 0).astype(jnp.int32)


def block_scale(own_key, dims, shards, least, largest):
    level = 1.0
    for position, parts in shards:
        steps = jax.random.uniform(jax.random.fold_in(jax.random.fold_in(own_key, 6), position), (parts,), jnp.float32, least / len(shards), largest / len(shards))
        level = level * jnp.repeat(jnp.exp(steps), dims[position] // parts).reshape((-1,) + (1,) * (len(dims) - 1 - position))
    return level


def gaussian(key, shape, scale, limit, pieces=(), kind=jnp.bfloat16):
    drawn = jax.random.normal(key, shape, jnp.float32) * scale
    if len(pieces) > 0:
        drawn = block_scale(key, shape, pieces, -0.22, 0.18) * drawn
    return jnp.clip(drawn, min=-limit, max=limit).astype(kind)


def setup_inputs(seed: int = 0) -> dict:
    key_list = jax.random.split(jax.random.key(seed), 5)
    return {
        "particle_data": draw_particle_data(jax.random.fold_in(key_list[4], 71), 0),
        "particle_cells": draw_particle_cells(jax.random.fold_in(key_list[4], 71), 0),
        "slot_counts": draw_slot_counts(jax.random.fold_in(key_list[4], 71), 0),
        "fluid_velocity": gaussian(key_list[3], (3, NZ, NX, NY), 1.0, 6.0, ((2, 16), (3, 8)), jnp.float32),
    }


TIME_STEP = 0.1
SHIFT = 0.05


def neighbours(padded):
    return [padded[2:, 1:-1, 1:-1], padded[:-2, 1:-1, 1:-1], padded[1:-1, 2:, 1:-1],
            padded[1:-1, :-2, 1:-1], padded[1:-1, 1:-1, 2:], padded[1:-1, 1:-1, :-2]]


def face_weights(padded_eps):
    center = padded_eps[1:-1, 1:-1, 1:-1]
    return [2.0 * center * around / (center + around) for around in neighbours(padded_eps)]


def apply_operator(padded, weights, diagonal):
    result = diagonal * padded[1:-1, 1:-1, 1:-1]
    for weight_face, value_face in zip(weights, neighbours(padded)):
        result = result - weight_face * value_face
    return result


def differences(padded):
    along_z = (padded[2:, 1:-1, 1:-1] - padded[:-2, 1:-1, 1:-1]) * 0.5
    along_x = (padded[1:-1, 2:, 1:-1] - padded[1:-1, :-2, 1:-1]) * 0.5
    along_y = (padded[1:-1, 1:-1, 2:] - padded[1:-1, 1:-1, :-2]) * 0.5
    return along_x, along_y, along_z


def reference(particle_data, particle_cells, slot_counts, fluid_velocity):
    depth, rows_x, rows_y = fluid_velocity.shape[1:]
    device_count = N_GX * N_GY
    capacity = particle_data.shape[3]
    slot_ids = jnp.arange(capacity, dtype=jnp.int32)
    occupied = (slot_ids[None, None, :] < slot_counts[:, :, None]).astype(jnp.float32)
    live = particle_data * occupied[None]
    owners = jnp.arange(device_count, dtype=jnp.int32)
    box_x = owners // N_GY
    box_y = owners % N_GY
    depth_pos = particle_cells[0]
    remainder = particle_cells[1]
    column_x = remainder // CY + box_x[None, :, None] * CX
    column_y = remainder % CY + box_y[None, :, None] * CY
    cell_index = ((depth_pos * rows_x + column_x) * rows_y + column_y).reshape(-1)
    volume = live[0]
    coefficient = live[1]
    velocity = live[2:5]
    deposit_terms = jnp.stack([volume, coefficient, coefficient * velocity[0],
                               coefficient * velocity[1], coefficient * velocity[2]]).reshape(5, -1)
    deposited = jnp.zeros((5, depth * rows_x * rows_y), jnp.float32).at[:, cell_index].add(deposit_terms)
    deposited = deposited.reshape(5, depth, rows_x, rows_y)
    fraction = deposited[0]
    porosity = 1.0 / (1.0 + fraction)
    predicted = fluid_velocity + TIME_STEP * (1.0 + fraction)[None] * (deposited[2:5] - deposited[1][None] * fluid_velocity)
    fluxes = porosity[None] * predicted
    weights = face_weights(jnp.pad(porosity, 1))
    diagonal = SHIFT * porosity
    for weight_face in weights:
        diagonal = diagonal + weight_face
    source_term = -(differences(jnp.pad(fluxes[0], 1))[0] + differences(jnp.pad(fluxes[1], 1))[1]
                    + differences(jnp.pad(fluxes[2], 1))[2])
    pressure = jnp.zeros_like(porosity)
    residual = source_term
    scaled = residual / diagonal
    direction = scaled
    norm_now = jnp.sum(residual * scaled)
    for iteration in range(ITERS):
        product_field = apply_operator(jnp.pad(direction, 1), weights, diagonal)
        step_length = norm_now / jnp.sum(direction * product_field)
        pressure = pressure + step_length * direction
        if iteration + 1 < ITERS:
            residual = residual - step_length * product_field
            scaled = residual / diagonal
            norm_next = jnp.sum(residual * scaled)
            direction = scaled + (norm_next / norm_now) * direction
            norm_now = norm_next
    gradient = differences(jnp.pad(pressure, 1))
    cell_table = jnp.stack([predicted[0], predicted[1], predicted[2],
                            gradient[0], gradient[1], gradient[2]]).reshape(6, -1)
    at_particles = cell_table[:, cell_index].reshape(6, device_count, device_count, capacity)
    forces = coefficient[None] * (at_particles[0:3] - velocity) - volume[None] * at_particles[3:6]
    return pressure, forces
```

```python
import functools
import jax
import jax.numpy as jnp
from jax import lax
from jax.experimental import pallas as pl
from jax.experimental.pallas import tpu as pltpu
from jax.sharding import PartitionSpec as P

f32, bf16, i32 = jnp.float32, jnp.bfloat16, jnp.int32
CH = 24
BR = 152
WL = 16
NW = 32
SPAN = WL * 128
VM = pltpu.CompilerParams(vmem_limit_bytes=56 * 1024 * 1024)


def sort_network(x):
    lane = lax.broadcasted_iota(i32, (1, 8, 128), 2)
    flipped = None
    for merge in range(1, 13):
        if merge < 12:
            if merge >= 5:
                want = (lane >> (merge - 5)) & 1
                mask = -want
            else:
                mask = jnp.asarray(-((lax.broadcasted_iota(i32, (32, 8, 128), 0) >> merge) & 1))
        else:
            mask = None
        if mask is not None:
            x = x ^ mask
        for bit in range(merge - 1, -1, -1):
            if bit < 5:
                step = 1 << bit
                y = x.reshape(32 // (2 * step), 2, step, 8, 128)
                a, b = y[:, 0], y[:, 1]
                x = jnp.stack([jnp.minimum(a, b), jnp.maximum(a, b)], axis=1).reshape(32, 8, 128)
            else:
                step = 1 << (bit - 5)
                up = (lane & step) != 0
                other = jnp.where(up, pltpu.roll(x, step, 2), pltpu.roll(x, 128 - step, 2))
                x = jnp.where(up, jnp.maximum(x, other), jnp.minimum(x, other))
        if mask is not None:
            x = x ^ mask
    return x


def lanes_to_chunks(x):
    lane = lax.broadcasted_iota(i32, (1, 8, 128), 2)
    for bit in range(5):
        step = 1 << bit
        y = x.reshape(32 // (2 * step), 2, step, 8, 128)
        a, b = y[:, 0], y[:, 1]
        up = ((lane & step) != 0)[:, None]
        na = jnp.where(up, pltpu.roll(b, step, 3), a)
        nb = jnp.where(up, b, pltpu.roll(a, 128 - step, 3))
        x = jnp.stack([na, nb], axis=1).reshape(32, 8, 128)
    for bit in range(2):
        step, far = 1 << bit, 32 << bit
        y = x.reshape(32 // (2 * step), 2, step, 8, 128)
        a, b = y[:, 0], y[:, 1]
        up = ((lane & far) != 0)[:, None]
        na = jnp.where(up, pltpu.roll(b, far, 3), a)
        nb = jnp.where(up, b, pltpu.roll(a, 128 - far, 3))
        x = jnp.stack([na, nb], axis=1).reshape(32, 8, 128)
    return jnp.stack([x[(c % 8) * 4 + c // 8] for c in range(32)], axis=0)


GROUPS = (((-2, -1, 0, 3), (2, -1, 3, 3), (0, -1, 6, 2)), ((-1, -1, 0, 3), (1, -1, 3, 3), (0, 1, 6, 1)))
NGX, NGY = 16, 8


def row_mask(first, count):
    row = lax.broadcasted_iota(i32, (8, 128), 0)
    return (row >= first) & (row < first + count)


def sort_kernel(runs, n_out, data_ref, cells_ref, counts_ref, *rest):
    outs, pos_ref = rest[:n_out], rest[n_out]
    data_v, cells_v, key_s, pay_s, out_s, sems = rest[n_out + 1:]
    hx, hy = lax.axis_index("gx"), lax.axis_index("gy")
    copies = []
    for t, (dx, _, _, _) in enumerate(runs):
        tile = pl.ds(pl.multiple_of(jnp.clip(hx + dx, 0, NGX - 1) * 8, 8), 8)
        copies.append(pltpu.make_async_copy(data_ref.at[:, 0, tile, :], data_v.at[t], sems.at[2 * t]))
        copies.append(pltpu.make_async_copy(cells_ref.at[:, 0, tile, :], cells_v.at[t], sems.at[2 * t + 1]))
    for copy in copies:
        copy.start()
    lane = lax.broadcasted_iota(i32, (8, 128), 1)
    row = lax.broadcasted_iota(i32, (8, 128), 0)
    counts = jnp.zeros((8, 128), i32)
    for dx, dy0, first, count in runs:
        for i in range(count):
            bx, by = hx + dx, hy + dy0 + i
            valid = (bx >= 0) & (bx < NGX) & (by >= 0) & (by < NGY)
            n = counts_ref[0, jnp.clip(bx * NGY + by, 0, NGX * NGY - 1)]
            counts = jnp.where(row == first + i, jnp.where(valid, n, 0), counts)
    shifts = [lax.rem(first - (hy + dy0) + 16, 8) for _, dy0, first, _ in runs]
    masks = [row_mask(first, count) for _, _, first, count in runs]
    for copy in copies:
        copy.wait()

    def gathered(ref, f, c):
        got = None
        for t in range(len(runs)):
            x = pltpu.roll(ref[t, f, :, c * 128:(c + 1) * 128], shifts[t], 0)
            got = x if got is None else jnp.where(masks[t], x, got)
        return got

    rows = []
    for c in range(32):
        slot = lane + c * 128
        if c < CH:
            h, col = gathered(cells_v, 0, c), gathered(cells_v, 1, c)
            live = slot < counts
            cell = (((col >> 7) * 64 + h) << 7) + (col & 127)
            cell = jnp.where(live, cell, 65536)
            for f in range(5):
                pay_s[f, c] = jnp.where(live, gathered(data_v, f, c), 0.0)
            rows.append((cell << 12) + slot)
        else:
            rows.append((1 << 29) + slot)
    keys = lanes_to_chunks(sort_network(jnp.stack(rows, axis=0)))
    key_s[...] = keys[:CH]
    place = lax.broadcasted_iota(i32, (32, 8, 128), 0) * 128 + lax.broadcasted_iota(i32, (32, 8, 128), 2)
    pad = lax.broadcasted_iota(i32, (32, 8, 128), 0) >= CH
    back = jnp.where(pad, (1 << 29) + place, ((keys & 4095) << 12) + place)
    back = lanes_to_chunks(sort_network(back))
    pos_ref[...] = back[:CH] & 4095

    def chunk(c, _):
        k = key_s[c]
        slot = k & 4095
        at, src = slot & 127, slot >> 7
        acc = [jnp.zeros((8, 128), f32) for _ in range(5)]
        for v in range(CH):
            here = src == v
            for f in range(5):
                got = jnp.take_along_axis(pay_s[f, v], at, axis=1)
                acc[f] = jnp.where(here, got, acc[f])
        for f in range(5):
            out_s[pl.ds(f * CH + c, 8, stride=BR), :] = acc[f]
        out_s[pl.ds(5 * CH + c, 8, stride=BR), :] = (k >> 12).astype(f32)
        return 0
    lax.fori_loop(0, CH, chunk, 0)
    low = lane < 64
    bound = jnp.where(low, lane, lane - 63) * SPAN
    total = jnp.zeros((8, 128), i32)
    for c in range(CH):
        cell = key_s[c] >> 12
        last = jnp.broadcast_to(cell[:, 127:128], (8, 128))
        start = jnp.broadcast_to(cell[:, 0:1], (8, 128))
        total = total + jnp.where(jnp.where(low, last, start) < bound, 1, 0)
    for r in range(8):
        out_s[pl.ds(6 * CH + r, 8, stride=BR), :] = total.astype(f32)
    for out, (_, _, first, count) in zip(outs, runs):
        out[...] = out_s[first * BR:(first + count) * BR, :]


def sort_blocks(runs, data, cells, counts):
    shapes = [jax.ShapeDtypeStruct((count * BR, 128), f32) for _, _, _, count in runs]
    shapes.append(jax.ShapeDtypeStruct((CH, 8, 128), i32))
    n = len(runs)
    return pl.pallas_call(
        functools.partial(sort_kernel, runs, n),
        out_shape=tuple(shapes),
        in_specs=[pl.BlockSpec(memory_space=pl.ANY)] * 2 + [pl.BlockSpec(memory_space=pltpu.SMEM)],
        out_specs=(pl.BlockSpec(memory_space=pltpu.VMEM),) * (n + 1),
        scratch_shapes=[
            pltpu.VMEM((n, 5, 8, 3072), f32),
            pltpu.VMEM((n, 2, 8, 3072), i32),
            pltpu.VMEM((CH, 8, 128), i32),
            pltpu.VMEM((5, CH, 8, 128), f32),
            pltpu.VMEM((8 * BR, 128), f32),
            pltpu.SemaphoreType.DMA((2 * n,)),
        ],
        compiler_params=VM,
        name="sort_blocks",
    )(data, cells, counts)


def load_offsets(refs, off_v, off_s, sem):
    for j, (ref, base) in enumerate(refs):
        off_v[j:j + 1, :] = ref[base + 6 * CH:base + 6 * CH + 1, :].astype(i32)
    copy = pltpu.make_async_copy(off_v, off_s, sem)
    copy.start()
    copy.wait()


def wide(row, rows):
    return jnp.broadcast_to(row, (rows, 128))


def split_cell(cell):
    line = jnp.floor(cell * (1.0 / 128.0))
    return line, cell - line * 128.0


def width_onehot(wid, iota):
    w16 = wide(wid, 16).astype(bf16)
    w = jnp.concatenate([w16] * 8, axis=0)
    return jnp.where(w == iota, jnp.asarray(1.0, bf16), jnp.asarray(0.0, bf16))


def deposit_kernel(nref, per, use_acc, *refs):
    bases = per
    blocks = [(refs[i], b) for i in range(nref) for b in bases]
    nb = len(blocks)
    rest = refs[nref:]
    if use_acc:
        prev, rest = rest[0], rest[1:]
    out, pre, off_v, off_s, sem = rest
    load_offsets(blocks, off_v, off_s, sem)
    for j, (ref, base) in enumerate(blocks):
        vol = ref[base:base + CH, :]
        coef = ref[base + CH:base + 2 * CH, :]
        vals = [vol, coef] + [coef * ref[base + (2 + d) * CH:base + (3 + d) * CH, :] for d in range(3)]
        for k, v in enumerate(vals):
            hi = v.astype(bf16).astype(f32)
            pre[j, k] = hi
            pre[j, 5 + k] = v - hi
        line, wid = split_cell(ref[base + 5 * CH:base + 6 * CH, :])
        pre[j, 10] = line
        pre[j, 11] = wid
    iota = lax.broadcasted_iota(i32, (128, 128), 0).astype(f32).astype(bf16)
    iota16 = lax.broadcasted_iota(i32, (16, 128), 0).astype(f32).astype(bf16)
    zero = jnp.zeros((16, 128), bf16)

    def operands(j, c, w):
        rel = jnp.clip(pre[j, 10, pl.ds(c, 1), :] - (w * WL).astype(f32), -1.0, 16.0)
        mask = wide(rel, 16).astype(bf16) == iota16
        a = jnp.concatenate(
            [jnp.where(mask, wide(pre[j, k, pl.ds(c, 1), :], 16).astype(bf16), zero) for k in range(10)], axis=0)
        return a, width_onehot(pre[j, 11, pl.ds(c, 1), :], iota)

    def product(a, b):
        return lax.dot_general(a, b, (((1,), (1,)), ((), ())), preferred_element_type=f32)

    def window(w, _):
        total = None
        more = 0
        for j in range(nb):
            first = jnp.minimum(off_s[j, w], CH - 2)
            more = jnp.maximum(more, off_s[j, 64 + w] - first)
            a0, b0 = operands(j, first, w)
            a1, b1 = operands(j, first + 1, w)
            p = product(jnp.concatenate([a0, a1], axis=1), jnp.concatenate([b0, b1], axis=1))
            total = p if total is None else total + p
        total = (total[:80] + total[80:]).reshape(5, WL, 128)
        rows = pl.ds(pl.multiple_of(w * WL, WL), WL)
        if use_acc:
            total = total + prev[:, rows, :]
        out[:, rows, :] = total

        @pl.when(more > 2)
        def _():
            def block(j, _):
                def step(c, _):
                    a, b = operands(j, c, w)
                    p = product(a, b)
                    out[:, rows, :] += (p[:80] + p[80:]).reshape(5, WL, 128)
                    return 0
                return lax.fori_loop(jnp.minimum(off_s[j, w], CH - 2) + 2, off_s[j, 64 + w], step, 0)
            lax.fori_loop(0, nb, block, 0)
        return 0
    lax.fori_loop(0, NW, window, 0)


def deposit(arrays, bases, prev=None):
    nb = len(arrays) * len(bases)
    args = list(arrays) + ([] if prev is None else [prev])
    return pl.pallas_call(
        functools.partial(deposit_kernel, len(arrays), bases, prev is not None),
        out_shape=jax.ShapeDtypeStruct((5, 512, 128), f32),
        in_specs=[pl.BlockSpec(memory_space=pltpu.VMEM)] * len(args),
        out_specs=pl.BlockSpec(memory_space=pltpu.VMEM),
        scratch_shapes=[
            pltpu.VMEM((nb, 12, CH, 128), f32),
            pltpu.VMEM((nb, 128), i32),
            pltpu.SMEM((nb, 128), i32),
            pltpu.SemaphoreType.DMA,
        ],
        compiler_params=VM,
        name="deposit",
    )(*args)


def interp_kernel(nref, bases, *refs):
    blocks = [(refs[i], b) for i in range(nref) for b in bases]
    nb = len(blocks)
    table, out, pre, acc, off_v, off_s, sem = refs[nref:]
    load_offsets(blocks, off_v, off_s, sem)
    for j, (ref, base) in enumerate(blocks):
        line, wid = split_cell(ref[base + 5 * CH:base + 6 * CH, :])
        pre[j, 0] = line
        pre[j, 1] = wid
    acc[...] = jnp.zeros_like(acc)
    iota = lax.broadcasted_iota(i32, (128, 128), 0).astype(f32).astype(bf16)
    iota16 = lax.broadcasted_iota(i32, (16, 128), 0).astype(f32)

    def visit(j, c, w, width, tab):
        masks, hots = [], []
        for i in range(width):
            rel = pre[j, 0, pl.ds(c + i, 1), :] - (w * WL).astype(f32)
            masks.append(wide(rel, 16) == iota16)
            b = width_onehot(pre[j, 1, pl.ds(c + i, 1), :], iota)
            hots.append(jnp.concatenate([b, b], axis=0))
        hot = hots[0] if width == 1 else jnp.concatenate(hots, axis=1)
        g = jnp.dot(tab, hot, preferred_element_type=f32)
        for i in range(width):
            for k in range(3):
                part = jnp.where(masks[i], g[k * 16:k * 16 + 16, i * 128:(i + 1) * 128], 0.0)
                acc[j, c + i, k] += part[:8] + part[8:]

    def window(w, _):
        tab = table[w]
        more = 0
        for j in range(nb):
            first = jnp.minimum(off_s[j, w], CH - 2)
            more = jnp.maximum(more, off_s[j, 64 + w] - first)
            visit(j, first, w, 2, tab)

        @pl.when(more > 2)
        def _():
            def block(j, _):
                def step(c, _):
                    visit(j, c, w, 1, tab)
                    return 0
                return lax.fori_loop(jnp.minimum(off_s[j, w], CH - 2) + 2, off_s[j, 64 + w], step, 0)
            lax.fori_loop(0, nb, block, 0)
        return 0
    lax.fori_loop(0, NW, window, 0)
    def fin(j, _):
        for k in range(3):
            out[j, k] = jnp.sum(acc[j, :, k], axis=1)
        return 0
    lax.fori_loop(0, nb, fin, 0)


def interp(arrays, bases, table):
    nb = len(arrays) * len(bases)
    args = list(arrays) + [table]
    return pl.pallas_call(
        functools.partial(interp_kernel, len(arrays), bases),
        out_shape=jax.ShapeDtypeStruct((nb, 3, CH, 128), f32),
        in_specs=[pl.BlockSpec(memory_space=pltpu.VMEM)] * len(args),
        out_specs=pl.BlockSpec(memory_space=pltpu.VMEM),
        scratch_shapes=[
            pltpu.VMEM((nb, 2, CH, 128), f32),
            pltpu.VMEM((nb, CH, 3, 8, 128), f32),
            pltpu.VMEM((nb, 128), i32),
            pltpu.SMEM((nb, 128), i32),
            pltpu.SemaphoreType.DMA,
        ],
        compiler_params=VM,
        name="interp",
    )(*args)


TIME_STEP = 0.1
SHIFT = 0.05
VSPEC = pl.BlockSpec(memory_space=pltpu.VMEM)
S = jax.ShapeDtypeStruct


def put_table(table, k, x, values):
    hi = values.astype(bf16)
    lo = (values - hi.astype(f32)).astype(bf16)
    for q in range(4):
        table[4 * x + q, k * 16:k * 16 + 16, 0:128] = hi[16 * q:16 * q + 16]
        table[4 * x + q, k * 16:k * 16 + 16, 128:256] = lo[16 * q:16 * q + 16]


def fields_kernel(acc, fluid, table, low, high):
    for x in range(8):
        at = slice(x * 64, x * 64 + 64)
        fraction = acc[0, at, :]
        drag = acc[1, at, :]
        porosity = 1.0 / (1.0 + fraction)
        out, r = (low, x) if x < 4 else (high, x - 4)
        out[0, r] = porosity
        for d in range(3):
            fluid_d = fluid[d, pl.ds(x, 64, stride=8), :]
            predicted = fluid_d + TIME_STEP * (1.0 + fraction) * (acc[2 + d, at, :] - drag * fluid_d)
            put_table(table, d, x, predicted)
            out[1 + d, r] = porosity * predicted


def fields(acc, fluid):
    return pl.pallas_call(
        fields_kernel,
        out_shape=(S((NW, 48, 256), bf16), S((4, 4, 64, 128), f32), S((4, 4, 64, 128), f32)),
        in_specs=[VSPEC] * 2,
        out_specs=(VSPEC,) * 3,
        compiler_params=VM,
        name="fields",
    )(acc, fluid)


def pack_kernel(left, low, high, right, out):
    lane = lax.broadcasted_iota(i32, (64, 128), 1)
    for f in range(4):
        got = jnp.zeros((64, 128), f32)
        for r in range(16):
            src = (left, low, high, right)[r // 4][f, r % 4]
            place = lax.rem(lane + 132 - 8 * r, 128) < 8
            got = jnp.where(place, src if r == 0 else pltpu.roll(src, 8 * r, 1), got)
        out[f] = got


def pack_edges(left, low, high, right):
    return pl.pallas_call(
        pack_kernel,
        out_shape=S((4, 64, 128), f32),
        in_specs=[VSPEC] * 4,
        out_specs=VSPEC,
        compiler_params=VM,
        name="pack_edges",
    )(left, low, high, right)


def up_z(x):
    return jnp.concatenate([x[1:], jnp.zeros_like(x[:1])], axis=0)


def down_z(x):
    return jnp.concatenate([jnp.zeros_like(x[:1]), x[:-1]], axis=0)


def up_y(x):
    return pltpu.roll(x, x.shape[1] - 1, 1)


def down_y(x):
    return pltpu.roll(x, 1, 1)


def face(e, n):
    return 2.0 * e * n / jnp.maximum(e + n, 1e-30)


def sweeps_kernel(left, low, high, right, from_left, from_right, vs, moments, ext, wx, wy, wz, diag, inv, src, more):
    lane = lax.broadcasted_iota(i32, (64, 128), 1)
    even = (lane & 7) < 4
    keep = (lane < 4) | (lane >= 124)
    for f in range(4):
        both = jnp.where(even, from_right[f], from_left[f])
        for r in range(16):
            ext[f, r, :, 0:128] = (left, low, high, right)[r // 4][f, r % 4]
            ext[f, r, :, 128:256] = jnp.where(keep, both if r == 0 else pltpu.roll(both, 128 - 8 * r, 1), 0.0)

    def faces(r, _):
        e = ext[0, r]
        wx[r] = face(e, ext[0, jnp.minimum(r + 1, 15)])
        wy[r] = face(e, up_y(e))
        wz[r] = face(e, up_z(e))
        return 0
    lax.fori_loop(0, 16, faces, 0)

    def sources(r, _):
        e = ext[0, r]
        y, z = wy[r], wz[r]
        d = SHIFT * e + wz[r] + down_z(z) + wx[r] + wx[r - 1] + y + down_y(y)
        outside = e == 0.0
        i = jnp.where(outside, 0.0, 1.0 / jnp.where(outside, 1.0, d))
        fy, fz = ext[2, r], ext[3, r]
        b = -0.5 * ((ext[1, r + 1] - ext[1, r - 1]) + (up_y(fy) - down_y(fy)) + (up_z(fz) - down_z(fz)))
        diag[r] = d
        inv[r] = i
        vs[0, r] = b * i
        return 0
    lax.fori_loop(1, 15, sources, 0)

    def spread(k, r):
        v = vs[k, r]
        y, z = wy[r], wz[r]
        total = wx[r] * vs[k, r + 1] + wx[r - 1] * vs[k, r - 1]
        total = total + y * up_y(v) + down_y(y * v)
        total = total + z * up_z(v) + down_z(z * v)
        return (diag[r] * v - total) * inv[r]

    for k, (lo, hi) in ((0, (2, 14)), (1, (3, 13))):
        def image(r, _, k=k):
            vs[k + 1, r] = spread(k, r)
            return 0
        lax.fori_loop(lo, hi, image, 0)

    def sums(r, total):
        d = diag[r][:, 0:128]
        v0, v1, v2 = (vs[k, r][:, 0:128] for k in range(3))
        v3 = spread(2, r)[:, 0:128]
        d0, d1, d2 = d * v0, d * v1, d * v2
        terms = (d0 * v0, d0 * v1, d1 * v1, d1 * v2, d2 * v2, d2 * v3)
        return tuple(t + jnp.sum(x.reshape(8, 8, 128), axis=0) for t, x in zip(total, terms))
    total = lax.fori_loop(4, 12, sums, tuple(jnp.zeros((8, 128), f32) for _ in range(6)))
    for k in range(6):
        moments[k:k + 1, :] = jnp.sum(total[k], axis=0, keepdims=True)
    moments[6:8, :] = jnp.zeros((2, 128), f32)


def sweeps(left, low, high, right, from_left, from_right):
    big = pltpu.VMEM((16, 64, 256), f32)
    return pl.pallas_call(
        sweeps_kernel,
        out_shape=(S((3, 16, 64, 256), f32), S((8, 128), f32)),
        in_specs=[VSPEC] * 6,
        out_specs=(VSPEC,) * 2,
        scratch_shapes=[pltpu.VMEM((4, 16, 64, 256), f32)] + [big] * 7,
        compiler_params=VM,
        name="sweeps",
    )(left, low, high, right, from_left, from_right)


def coefficients(mu):
    def form(a, b, shift):
        return sum(a[i] * b[j] * mu[i + j + shift] for i in range(len(a)) for j in range(len(b)))
    zero = jnp.zeros_like(mu[0])
    one = jnp.ones_like(mu[0])
    pressure = [zero, zero, zero]
    scaled, direction = [one], [one]
    norm = mu[0]
    for sweep in range(3):
        step = norm / form(direction, direction, 1)
        for i, c in enumerate(direction):
            pressure[i] = pressure[i] + step * c
        if sweep < 2:
            moved = [zero] + direction
            old = scaled + [zero] * (len(moved) - len(scaled))
            scaled = [a - step * b for a, b in zip(old, moved)]
            following = form(scaled, scaled, 0)
            ratio = following / norm
            direction = [a + ratio * b for a, b in zip(scaled, direction + [zero])]
            norm = following
    return pressure


def gradient_kernel(all_moments, vs, pressure, table, p):
    summed = jnp.sum(all_moments[...], axis=0)
    mu = [jnp.broadcast_to(jnp.sum(summed[k:k + 1, :], axis=1, keepdims=True), (8, 256)) for k in range(6)]
    coef = [jnp.broadcast_to(c[:1], (64, 256)) for c in coefficients(mu)]

    def combine(r, _):
        p[r] = coef[0] * vs[0, r] + coef[1] * vs[1, r] + coef[2] * vs[2, r]
        return 0
    lax.fori_loop(3, 13, combine, 0)
    for x in range(8):
        here = p[x + 4]
        core = here[:, 0:128]
        pressure[pl.ds(x, 64, stride=8), :] = core
        put_table(table, 0, x, 0.5 * (p[x + 5][:, 0:128] - p[x + 3][:, 0:128]))
        put_table(table, 1, x, 0.5 * (up_y(here) - down_y(here))[:, 0:128])
        put_table(table, 2, x, 0.5 * (up_z(core) - down_z(core)))


def gradients(all_moments, vs):
    return pl.pallas_call(
        gradient_kernel,
        out_shape=(S((512, 128), f32), S((NW, 48, 256), bf16)),
        in_specs=[VSPEC] * 2,
        out_specs=(VSPEC,) * 2,
        scratch_shapes=[pltpu.VMEM((16, 64, 256), f32)],
        compiler_params=VM,
        name="gradients",
    )(all_moments, vs)


PR = 3 * CH


def place_kernel(back_refs, groups, *refs):
    n = back_refs
    backs, (pos_a, pos_b), out = refs[:n], refs[n:n + 2], refs[n + 2]
    stage, found, tiles, zeros, sem_zero, sem_tile = refs[n + 3:]
    hx, hy = lax.axis_index("gx"), lax.axis_index("gy")
    zeros[...] = jnp.zeros_like(zeros)

    def tile_at(t):
        return out.at[:, 0, pl.ds(pl.multiple_of(t * 8, 8), 8), :]

    def far(t):
        return jnp.abs(t - hx) > 2
    for t in range(16):
        @pl.when(far(t))
        def _():
            pltpu.make_async_copy(zeros, tile_at(t), sem_zero.at[t]).start()
    where = {-2: 0, -1: 1, 0: 2, 1: 3, 2: 4}
    for g, runs in enumerate(groups):
        for dx, dy0, first, count in runs:
            for i in range(count):
                src = (dy0 + i + 1) * PR
                stage[(first + i) * PR:(first + i + 1) * PR, :] = backs[where[dx]][src:src + PR, :]
        if g == 1:
            stage[7 * PR:8 * PR, :] = jnp.zeros((PR, 128), f32)
        pos_ref = (pos_a, pos_b)[g]

        def chunk(c, _):
            k = pos_ref[c]
            at, src = k & 127, k >> 7
            acc = [jnp.zeros((8, 128), f32) for _ in range(3)]
            for v in range(CH):
                here = src == v
                for f in range(3):
                    got = jnp.take_along_axis(stage[pl.ds(f * CH + v, 8, stride=PR), :], at, axis=1)
                    acc[f] = jnp.where(here, got, acc[f])
            for f in range(3):
                found[g, f, c] = acc[f]
            return 0
        lax.fori_loop(0, CH, chunk, 0)
    row = lax.broadcasted_iota(i32, (8, 128), 0)
    for dx in (-2, -1, 0, 1, 2):
        pieces = [(g, run) for g, runs in enumerate(groups) for run in runs if run[0] == dx]
        turned = []
        for g, (_, dy0, first, count) in pieces:
            shift = lax.rem(hy + dy0 - first + 16, 8)
            low = hy + dy0
            turned.append((g, shift, (row >= low) & (row < low + count)))
        for f in range(3):
            for c in range(CH):
                got = jnp.zeros((8, 128), f32)
                for g, shift, mask in turned:
                    got = jnp.where(mask, pltpu.roll(found[g, f, c], shift, 0), got)
                tiles[where[dx], f, :, c * 128:(c + 1) * 128] = got

        @pl.when((hx + dx >= 0) & (hx + dx < NGX))
        def _():
            pltpu.make_async_copy(tiles.at[where[dx]], tile_at(hx + dx), sem_tile.at[where[dx]]).start()
    for t in range(16):
        @pl.when(far(t))
        def _():
            pltpu.make_async_copy(zeros, tile_at(t), sem_zero.at[t]).wait()
    for dx in (-2, -1, 0, 1, 2):
        @pl.when((hx + dx >= 0) & (hx + dx < NGX))
        def _():
            pltpu.make_async_copy(tiles.at[where[dx]], tile_at(hx + dx), sem_tile.at[where[dx]]).wait()


def place_forces(backs, pos):
    return pl.pallas_call(
        functools.partial(place_kernel, len(backs), GROUPS),
        out_shape=S((3, 1, 128, 3072), f32),
        in_specs=[VSPEC] * (len(backs) + 2),
        out_specs=pl.BlockSpec(memory_space=pl.ANY),
        scratch_shapes=[
            pltpu.VMEM((8 * PR, 128), f32),
            pltpu.VMEM((2, 3, CH, 8, 128), f32),
            pltpu.VMEM((5, 3, 8, 3072), f32),
            pltpu.VMEM((3, 8, 3072), f32),
            pltpu.SemaphoreType.DMA((16,)),
            pltpu.SemaphoreType.DMA((5,)),
        ],
        compiler_params=VM,
        name="place_forces",
    )(*backs, *pos)


def force_kernel(nref, bases, *refs):
    blocks = [(refs[i], b) for i in range(nref) for b in bases]
    at_pred, at_grad, out = refs[nref:]
    for j, (ref, base) in enumerate(blocks):
        volume = ref[base:base + CH, :]
        coef = ref[base + CH:base + 2 * CH, :]
        for d in range(3):
            vel = ref[base + (2 + d) * CH:base + (3 + d) * CH, :]
            out[j * PR + d * CH:j * PR + (d + 1) * CH, :] = coef * (at_pred[j, d] - vel) - volume * at_grad[j, d]


def block_forces(arrays, bases, at_pred, at_grad):
    nb = len(arrays) * len(bases)
    return pl.pallas_call(
        functools.partial(force_kernel, len(arrays), bases),
        out_shape=S((nb * PR, 128), f32),
        in_specs=[VSPEC] * (len(arrays) + 2),
        out_specs=VSPEC,
        compiler_params=VM,
        name="block_forces",
    )(*arrays, at_pred, at_grad)


def pairs(count, by):
    return [(i, i + by) for i in range(count) if 0 <= i + by < count]


def shift_x(x, by):
    return lax.ppermute(x, "gx", pairs(NGX, by))


def shift_y(x, by):
    return lax.ppermute(x, "gy", pairs(NGY, by))


def per_device(particle_data, particle_cells, slot_counts, fluid_velocity):
    m2, p2, zero_a, pos_a = sort_blocks(GROUPS[0], particle_data, particle_cells, slot_counts)
    m1, p1, zero_b, pos_b = sort_blocks(GROUPS[1], particle_data, particle_cells, slot_counts)
    along = [
        shift_x(m2, -2),
        shift_x(m1, -1),
        jnp.concatenate([zero_a, zero_b], axis=0),
        shift_x(p1, 1),
        shift_x(p2, 2),
    ]
    parts = [jnp.concatenate([a[d * BR:(d + 1) * BR] for a in along], axis=0) for d in range(3)]
    mine = parts[1]
    sides = [shift_y(parts[0], -1), shift_y(parts[2], 1)]
    bases = tuple(range(0, 5 * BR, BR))
    acc = deposit([mine], bases)
    acc = deposit(sides, bases, acc)
    table, low, high = fields(acc, fluid_velocity.reshape(3, 512, 128))
    left, right = shift_x(high, 1), shift_x(low, -1)
    packed = pack_edges(left, low, high, right)
    from_left, from_right = shift_y(packed, 1), shift_y(packed, -1)
    vs, moments = sweeps(left, low, high, right, from_left, from_right)
    everyone = lax.all_to_all(jnp.broadcast_to(moments[None], (NGX * NGY, 8, 128)), ("gx", "gy"), 0, 0)
    blocks = [sides[0], mine, sides[1]]
    at_pred = [interp([b], bases, table) for b in blocks]
    pressure, slopes = gradients(everyone, vs)
    at_grad = [interp([b], bases, slopes) for b in blocks]
    forces = [block_forces([b], bases, p, g) for b, p, g in zip(blocks, at_pred, at_grad)]
    forces = [shift_y(forces[0], 1), forces[1], shift_y(forces[2], -1)]
    backs = []
    for i, dx in enumerate((-2, -1, 0, 1, 2)):
        block = jnp.concatenate([f[i * PR:(i + 1) * PR] for f in forces], axis=0)
        backs.append(block if dx == 0 else shift_x(block, -dx))
    drag = place_forces(backs, [pos_a, pos_b])
    return pressure.reshape(64, 8, 128), drag


def solution(mesh):
    return jax.shard_map(
        per_device,
        mesh=mesh,
        in_specs=(
            P(None, ("gx", "gy"), None, None),
            P(None, ("gx", "gy"), None, None),
            P(("gx", "gy"), None),
            P(None, None, "gx", "gy"),
        ),
        out_specs=(P(None, "gx", "gy"), P(None, ("gx", "gy"), None, None)),
        check_vma=False,
    )
```

```python
import functools
import jax
import jax.numpy as jnp
from jax import lax
from jax.experimental import pallas as pl
from jax.experimental.pallas import tpu as pltpu
from jax.sharding import PartitionSpec as P

f32, bf16, i32 = jnp.float32, jnp.bfloat16, jnp.int32
CH = 24
BR = 152
WL = 16
NW = 32
SPAN = WL * 128
PR = 3 * CH
VM = pltpu.CompilerParams(vmem_limit_bytes=56 * 1024 * 1024)
VSPEC = pl.BlockSpec(memory_space=pltpu.VMEM)
S = jax.ShapeDtypeStruct
TOKEN = S((8, 128), f32)


def sort_network(x):
    lane = lax.broadcasted_iota(i32, (1, 8, 128), 2)
    flipped = None
    for merge in range(1, 13):
        if merge < 12:
            if merge >= 5:
                want = (lane >> (merge - 5)) & 1
                mask = -want
            else:
                mask = jnp.asarray(-((lax.broadcasted_iota(i32, (32, 8, 128), 0) >> merge) & 1))
        else:
            mask = None
        if mask is not None:
            x = x ^ mask
        for bit in range(merge - 1, -1, -1):
            if bit < 5:
                step = 1 << bit
                y = x.reshape(32 // (2 * step), 2, step, 8, 128)
                a, b = y[:, 0], y[:, 1]
                x = jnp.stack([jnp.minimum(a, b), jnp.maximum(a, b)], axis=1).reshape(32, 8, 128)
            else:
                step = 1 << (bit - 5)
                up = (lane & step) != 0
                other = jnp.take_along_axis(x, jnp.broadcast_to(lane ^ step, x.shape), axis=2)
                x = jnp.where(up, jnp.maximum(x, other), jnp.minimum(x, other))
        if mask is not None:
            x = x ^ mask
    return x


def lanes_to_chunks(x):
    lane = lax.broadcasted_iota(i32, (1, 8, 128), 2)
    for bit in range(5):
        step = 1 << bit
        y = x.reshape(32 // (2 * step), 2, step, 8, 128)
        a, b = y[:, 0], y[:, 1]
        up = ((lane & step) != 0)[:, None]
        na = jnp.where(up, pltpu.roll(b, step, 3), a)
        nb = jnp.where(up, b, pltpu.roll(a, 128 - step, 3))
        x = jnp.stack([na, nb], axis=1).reshape(32, 8, 128)
    for bit in range(2):
        step, far = 1 << bit, 32 << bit
        y = x.reshape(32 // (2 * step), 2, step, 8, 128)
        a, b = y[:, 0], y[:, 1]
        up = ((lane & far) != 0)[:, None]
        na = jnp.where(up, pltpu.roll(b, far, 3), a)
        nb = jnp.where(up, b, pltpu.roll(a, 128 - far, 3))
        x = jnp.stack([na, nb], axis=1).reshape(32, 8, 128)
    return jnp.stack([x[(c % 8) * 4 + c // 8] for c in range(32)], axis=0)


GROUPS = (((-2, -1, 0, 3), (2, -1, 3, 3), (0, -1, 6, 2)), ((-1, -1, 0, 3), (1, -1, 3, 3), (0, 1, 6, 1)))
NGX, NGY = 16, 8


def row_mask(first, count):
    row = lax.broadcasted_iota(i32, (8, 128), 0)
    return (row >= first) & (row < first + count)


def sort_kernel(runs, n_out, data_ref, cells_ref, counts_ref, *rest):
    outs, pos_ref = rest[:n_out], rest[n_out]
    data_v, cells_v, key_s, pay_s, out_s, sems = rest[n_out + 1:]
    hx, hy = lax.axis_index("gx"), lax.axis_index("gy")
    copies = []
    for t, (dx, _, _, _) in enumerate(runs):
        tile = pl.ds(pl.multiple_of(jnp.clip(hx + dx, 0, NGX - 1) * 8, 8), 8)
        copies.append(pltpu.make_async_copy(data_ref.at[:, 0, tile, :], data_v.at[t], sems.at[2 * t]))
        copies.append(pltpu.make_async_copy(cells_ref.at[:, 0, tile, :], cells_v.at[t], sems.at[2 * t + 1]))
    for copy in copies:
        copy.start()
    lane = lax.broadcasted_iota(i32, (8, 128), 1)
    row = lax.broadcasted_iota(i32, (8, 128), 0)
    counts = jnp.zeros((8, 128), i32)
    for dx, dy0, first, count in runs:
        for i in range(count):
            bx, by = hx + dx, hy + dy0 + i
            valid = (bx >= 0) & (bx < NGX) & (by >= 0) & (by < NGY)
            n = counts_ref[0, jnp.clip(bx * NGY + by, 0, NGX * NGY - 1)]
            counts = jnp.where(row == first + i, jnp.where(valid, n, 0), counts)
    shifts = [lax.rem(first - (hy + dy0) + 16, 8) for _, dy0, first, _ in runs]
    masks = [row_mask(first, count) for _, _, first, count in runs]
    for copy in copies:
        copy.wait()

    def gathered(ref, f, c):
        got = None
        for t in range(len(runs)):
            x = pltpu.roll(ref[t, f, :, c * 128:(c + 1) * 128], shifts[t], 0)
            got = x if got is None else jnp.where(masks[t], x, got)
        return got

    rows = []
    for c in range(32):
        slot = lane + c * 128
        if c < CH:
            h, col = gathered(cells_v, 0, c), gathered(cells_v, 1, c)
            live = slot < counts
            cell = (((col >> 7) * 64 + h) << 7) + (col & 127)
            cell = jnp.where(live, cell, 65536)
            for f in range(5):
                pay_s[f, c] = jnp.where(live, gathered(data_v, f, c), 0.0)
            rows.append((cell << 12) + slot)
        else:
            rows.append((1 << 29) + slot)
    keys = lanes_to_chunks(sort_network(jnp.stack(rows, axis=0)))
    key_s[...] = keys[:CH]
    pos_ref[...] = keys[:CH]

    def chunk(c, _):
        k = key_s[c]
        slot = k & 4095
        at, src = slot & 127, slot >> 7
        acc = [jnp.zeros((8, 128), f32) for _ in range(5)]
        for v in range(CH):
            here = src == v
            for f in range(5):
                got = jnp.take_along_axis(pay_s[f, v], at, axis=1)
                acc[f] = jnp.where(here, got, acc[f])
        for f in range(5):
            out_s[pl.ds(f * CH + c, 8, stride=BR), :] = acc[f]
        out_s[pl.ds(5 * CH + c, 8, stride=BR), :] = (k >> 12).astype(f32)
        return 0
    lax.fori_loop(0, CH, chunk, 0)
    low = lane < 64
    bound = jnp.where(low, lane, lane - 63) * SPAN
    total = jnp.zeros((8, 128), i32)
    for c in range(CH):
        cell = key_s[c] >> 12
        last = jnp.broadcast_to(cell[:, 127:128], (8, 128))
        start = jnp.broadcast_to(cell[:, 0:1], (8, 128))
        total = total + jnp.where(jnp.where(low, last, start) < bound, 1, 0)
    for r in range(8):
        out_s[pl.ds(6 * CH + r, 8, stride=BR), :] = total.astype(f32)
    side = lax.rem(hx // abs(runs[0][0]), 2) == 0
    for out, first in ((outs[0], jnp.where(side, 3 * BR, 0)), (outs[1], jnp.where(side, 0, 3 * BR))):
        out[...] = out_s[pl.ds(pl.multiple_of(first, 8), 3 * BR), :]
    _, _, first, count = runs[2]
    outs[2][...] = out_s[first * BR:(first + count) * BR, :]


def inverse_kernel(keys_a, keys_b, after, pos_a, pos_b, token):
    token[...] = after[...]
    place = lax.broadcasted_iota(i32, (CH, 8, 128), 0) * 128 + lax.broadcasted_iota(i32, (CH, 8, 128), 2)
    rest = jnp.full((32 - CH, 8, 128), 1 << 29, i32)
    for keys, pos in ((keys_a, pos_a), (keys_b, pos_b)):
        back = jnp.concatenate([((keys[...] & 4095) << 12) + place, rest], axis=0)
        pos[...] = lanes_to_chunks(sort_network(back))[:CH] & 4095


def inverse(keys_a, keys_b, after):
    shape = jax.ShapeDtypeStruct((CH, 8, 128), i32)
    return pl.pallas_call(
        inverse_kernel,
        out_shape=(shape, shape, TOKEN),
        in_specs=[VSPEC] * 3,
        out_specs=(VSPEC,) * 3,
        compiler_params=VM,
        cost_estimate=pl.CostEstimate(flops=10**9, bytes_accessed=2 * 10**7, transcendentals=0),
        name="inverse",
    )(keys_a, keys_b, after)


def sort_blocks(runs, data, cells, counts):
    shapes = [jax.ShapeDtypeStruct((count * BR, 128), f32) for _, _, _, count in runs]
    shapes.append(jax.ShapeDtypeStruct((CH, 8, 128), i32))
    n = len(runs)
    return pl.pallas_call(
        functools.partial(sort_kernel, runs, n),
        out_shape=tuple(shapes),
        in_specs=[pl.BlockSpec(memory_space=pl.ANY)] * 2 + [pl.BlockSpec(memory_space=pltpu.SMEM)],
        out_specs=(pl.BlockSpec(memory_space=pltpu.VMEM),) * (n + 1),
        scratch_shapes=[
            pltpu.VMEM((n, 5, 8, 3072), f32),
            pltpu.VMEM((n, 2, 8, 3072), i32),
            pltpu.VMEM((CH, 8, 128), i32),
            pltpu.VMEM((5, CH, 8, 128), f32),
            pltpu.VMEM((8 * BR, 128), f32),
            pltpu.SemaphoreType.DMA((2 * n,)),
        ],
        compiler_params=VM,
        name="sort_blocks",
    )(data, cells, counts)


def load_offsets(refs, off_v, off_s, sem):
    for j, (ref, base) in enumerate(refs):
        off_v[j:j + 1, :] = ref[base + 6 * CH:base + 6 * CH + 1, :].astype(i32)
    copy = pltpu.make_async_copy(off_v, off_s, sem)
    copy.start()
    copy.wait()


def wide(row, rows):
    return jnp.broadcast_to(row, (rows, 128))


def split_cell(cell):
    line = jnp.floor(cell * (1.0 / 128.0))
    return line, cell - line * 128.0


def width_onehot(wid, iota):
    w16 = wide(wid, 16).astype(bf16)
    w = jnp.concatenate([w16] * 8, axis=0)
    return jnp.where(w == iota, jnp.asarray(1.0, bf16), jnp.asarray(0.0, bf16))


def deposit_kernel(nref, bases, unroll, use_acc, *refs):
    blocks = [(refs[i], b) for i in range(nref) for b in bases]
    nb = len(blocks)
    rest = refs[nref:]
    if use_acc:
        prev, fluid, table, own_0, own_1, token, out, pre, off_v, off_s, sem = rest
    else:
        out, pre, off_v, off_s, sem = rest
    load_offsets(blocks, off_v, off_s, sem)
    for j, (ref, base) in enumerate(blocks):
        vol = ref[base:base + CH, :]
        coef = ref[base + CH:base + 2 * CH, :]
        vals = [vol, coef] + [coef * ref[base + (2 + d) * CH:base + (3 + d) * CH, :] for d in range(3)]
        for k, v in enumerate(vals):
            hi = v.astype(bf16).astype(f32)
            pre[j, k] = hi
            pre[j, 5 + k] = v - hi
        line, wid = split_cell(ref[base + 5 * CH:base + 6 * CH, :])
        pre[j, 10] = line
        pre[j, 11] = wid
    iota = lax.broadcasted_iota(i32, (128, 128), 0).astype(f32).astype(bf16)
    iota16 = lax.broadcasted_iota(i32, (16, 128), 0).astype(f32).astype(bf16)
    zero = jnp.zeros((16, 128), bf16)

    def operands(j, c, w):
        rel = jnp.clip(pre[j, 10, pl.ds(c, 1), :] - (w * WL).astype(f32), -1.0, 16.0)
        mask = wide(rel, 16).astype(bf16) == iota16
        a = jnp.concatenate(
            [jnp.where(mask, wide(pre[j, k, pl.ds(c, 1), :], 16).astype(bf16), zero) for k in range(10)], axis=0)
        return a, width_onehot(pre[j, 11, pl.ds(c, 1), :], iota)

    def product(a, b):
        p = lax.dot_general(a, b, (((1,), (1,)), ((), ())), preferred_element_type=f32)
        return p

    def halves(p):
        return (p[:80] + p[80:]).reshape(5, WL, 128)

    def windows(i, more):
        for u in range(unroll):
            w = i * unroll + u
            total = None
            for j in range(nb):
                first = jnp.minimum(off_s[j, w], CH - 2)
                more = jnp.maximum(more, off_s[j, 64 + w] - first)
                a0, b0 = operands(j, first, w)
                a1, b1 = operands(j, first + 1, w)
                p = product(jnp.concatenate([a0, a1], axis=1), jnp.concatenate([b0, b1], axis=1))
                total = p if total is None else total + p
            total = halves(total)
            rows = pl.ds(pl.multiple_of(w * WL, WL), WL)
            if use_acc:
                total = total + prev[:, rows, :]
            out[:, rows, :] = total
        return more
    more = lax.fori_loop(0, NW // unroll, windows, jnp.int32(0))

    @pl.when(more > 2)
    def _():
        def window(w, _):
            rows = pl.ds(pl.multiple_of(w * WL, WL), WL)

            def block(j, _):
                def step(c, _):
                    a, b = operands(j, c, w)
                    out[:, rows, :] += halves(product(a, b))
                    return 0
                return lax.fori_loop(jnp.minimum(off_s[j, w], CH - 2) + 2, off_s[j, 64 + w], step, 0)
            return lax.fori_loop(0, nb, block, 0)
        lax.fori_loop(0, NW, window, 0)


    if use_acc:
        fields(out, fluid, table, own_0, own_1)
        token[...] = jnp.zeros_like(token)


def deposit(arrays, bases, unroll, prev=None, fluid=None):
    nb = len(arrays) * len(bases)
    args = list(arrays) + ([] if prev is None else [prev, fluid])
    total = S((5, 512, 128), f32)
    shapes = (S((NW, 48, 256), bf16), S((4, 4, 64, 128), f32), S((4, 4, 64, 128), f32), TOKEN)
    scratch = [
        pltpu.VMEM((nb, 12, CH, 128), f32),
        pltpu.VMEM((nb, 128), i32),
        pltpu.SMEM((nb, 128), i32),
        pltpu.SemaphoreType.DMA,
    ]
    if prev is not None:
        scratch = [pltpu.VMEM((5, 512, 128), f32)] + scratch
    return pl.pallas_call(
        functools.partial(deposit_kernel, len(arrays), bases, unroll, prev is not None),
        out_shape=total if prev is None else shapes,
        in_specs=[VSPEC] * len(args),
        out_specs=VSPEC if prev is None else (VSPEC,) * 4,
        scratch_shapes=scratch,
        compiler_params=VM,
        cost_estimate=pl.CostEstimate(flops=10**9 * nb, bytes_accessed=3 * 10**6 * nb, transcendentals=0),
        name="deposit",
    )(*args)


def interp_kernel(nref, bases, unroll, *refs):
    blocks = [(refs[i], b) for i in range(nref) for b in bases]
    nb = len(blocks)
    fast, slope, _ = refs[nref:nref + 3]
    outs = refs[nref + 3:-6]
    token, pre, acc, off_v, off_s, sem = refs[-6:]
    each = nb // len(outs)
    token[...] = jnp.zeros_like(token)
    load_offsets(blocks, off_v, off_s, sem)
    for j, (ref, base) in enumerate(blocks):
        line, wid = split_cell(ref[base + 5 * CH:base + 6 * CH, :])
        pre[j, 0] = line
        pre[j, 1] = wid
        pre[j, 2] = ref[base + CH:base + 2 * CH, :]
        pre[j, 3] = -ref[base:base + CH, :]
    acc[...] = jnp.zeros_like(acc)
    iota = lax.broadcasted_iota(i32, (128, 128), 0).astype(f32).astype(bf16)
    iota16 = lax.broadcasted_iota(i32, (16, 128), 0).astype(f32)

    def visit(j, c, w, width, tab):
        scales, hots = [], []
        for i in range(width):
            at = pl.ds(c + i, 1)
            mask = wide(pre[j, 0, at, :] - (w * WL).astype(f32), 16) == iota16
            scales.append([jnp.where(mask, wide(pre[j, 2 + s, at, :], 16), 0.0) for s in range(2)])
            b = width_onehot(pre[j, 1, at, :], iota)
            hots.append(jnp.concatenate([b, b], axis=0))
        hot = hots[0] if width == 1 else jnp.concatenate(hots, axis=1)
        g = jnp.dot(tab, hot, preferred_element_type=f32)
        for i in range(width):
            for k in range(3):
                lanes = slice(i * 128, (i + 1) * 128)
                part = scales[i][0] * g[k * 16:k * 16 + 16, lanes]
                part = part + scales[i][1] * g[48 + k * 16:64 + k * 16, lanes]
                acc[j, c + i, k] += part[:8] + part[8:]

    def windows(i, more):
        for u in range(unroll):
            w = i * unroll + u
            tab = jnp.concatenate([fast[w], slope[w]], axis=0)
            for j in range(nb):
                first = jnp.minimum(off_s[j, w], CH - 2)
                more = jnp.maximum(more, off_s[j, 64 + w] - first)
                visit(j, first, w, 2, tab)
        return more
    more = lax.fori_loop(0, NW // unroll, windows, jnp.int32(0))

    @pl.when(more > 2)
    def _():
        def window(w, _):
            tab = jnp.concatenate([fast[w], slope[w]], axis=0)

            def block(j, _):
                def step(c, _):
                    visit(j, c, w, 1, tab)
                    return 0
                return lax.fori_loop(jnp.minimum(off_s[j, w], CH - 2) + 2, off_s[j, 64 + w], step, 0)
            return lax.fori_loop(0, nb, block, 0)
        lax.fori_loop(0, NW, window, 0)
    for j, (ref, base) in enumerate(blocks):
        coef = ref[base + CH:base + 2 * CH, :]
        for k in range(3):
            vel = ref[base + (2 + k) * CH:base + (3 + k) * CH, :]
            at = (j % each) * PR + k * CH
            outs[j // each][at:at + CH, :] = jnp.sum(acc[j, :, k], axis=1) - coef * vel


def interp(arrays, bases, fast, slope, unroll, after, n_out):
    nb = len(arrays) * len(bases)
    args = list(arrays) + [fast, slope, after]
    return pl.pallas_call(
        functools.partial(interp_kernel, len(arrays), bases, unroll),
        out_shape=(S((nb // n_out * PR, 128), f32),) * n_out + (TOKEN,),
        in_specs=[VSPEC] * len(args),
        out_specs=(VSPEC,) * (n_out + 1),
        scratch_shapes=[
            pltpu.VMEM((nb, 4, CH, 128), f32),
            pltpu.VMEM((nb, CH, 3, 8, 128), f32),
            pltpu.VMEM((nb, 128), i32),
            pltpu.SMEM((nb, 128), i32),
            pltpu.SemaphoreType.DMA,
        ],
        compiler_params=VM,
        cost_estimate=pl.CostEstimate(flops=10**9 * nb, bytes_accessed=3 * 10**6 * nb, transcendentals=0),
        name="interp",
    )(*args)

TIME_STEP = 0.1
SHIFT = 0.05


def put_table(table, k, x, values):
    hi = values.astype(bf16)
    lo = (values - hi.astype(f32)).astype(bf16)
    for q in range(4):
        table[4 * x + q, k * 16:k * 16 + 16, 0:128] = hi[16 * q:16 * q + 16]
        table[4 * x + q, k * 16:k * 16 + 16, 128:256] = lo[16 * q:16 * q + 16]


def fields(acc, fluid, table, own_0, own_1):
    even = lax.rem(lax.axis_index("gx"), 2) == 0
    for r in range(4):
        made = []
        for x in (r, r + 4):
            at = slice(x * 64, x * 64 + 64)
            fraction = acc[0, at, :]
            drag = acc[1, at, :]
            porosity = 1.0 / (1.0 + fraction)
            values = [porosity]
            for d in range(3):
                fluid_d = fluid[d, pl.ds(x, 64, stride=8), :]
                predicted = fluid_d + TIME_STEP * (1.0 + fraction) * (acc[2 + d, at, :] - drag * fluid_d)
                put_table(table, d, x, predicted)
                values.append(porosity * predicted)
            made.append(values)
        for f in range(4):
            low, high = made[0][f], made[1][f]
            own_0[f, r] = jnp.where(even, high, low)
            own_1[f, r] = jnp.where(even, low, high)


def extended_row(rows, f, r, even):
    own_0, own_1, got_0, got_1 = rows
    first, second = ((got_1, got_0), (own_1, own_0), (own_0, own_1), (got_0, got_1))[r // 4]
    return jnp.where(even, first[f, r % 4], second[f, r % 4])


def pack_kernel(own_0, own_1, got_0, got_1, after, out):
    del after
    even = lax.rem(lax.axis_index("gx"), 2) == 0
    rows = (own_0, own_1, got_0, got_1)
    lane = lax.broadcasted_iota(i32, (64, 128), 1)
    for f in range(4):
        got = jnp.zeros((64, 128), f32)
        for r in range(16):
            src = extended_row(rows, f, r, even)
            place = lax.rem(lane + 132 - 8 * r, 128) < 8
            got = jnp.where(place, src if r == 0 else pltpu.roll(src, 8 * r, 1), got)
        out[f] = got


def pack_edges(rows, after):
    return pl.pallas_call(
        pack_kernel,
        out_shape=S((4, 64, 128), f32),
        in_specs=[VSPEC] * 5,
        out_specs=VSPEC,
        compiler_params=VM,
        name="pack_edges",
    )(*rows, after)


def up_z(x):
    return jnp.concatenate([x[1:], jnp.zeros_like(x[:1])], axis=0)


def down_z(x):
    return jnp.concatenate([jnp.zeros_like(x[:1]), x[:-1]], axis=0)


def up_y(x):
    return pltpu.roll(x, x.shape[1] - 1, 1)


def down_y(x):
    return pltpu.roll(x, 1, 1)


def face(e, n):
    return 2.0 * e * n / jnp.maximum(e + n, 1e-30)


def sweeps_kernel(own_0, own_1, got_0, got_1, edge_0, edge_1, vs, moments, ext, wx, wy, wz, diag, inv, src, more):
    lane = lax.broadcasted_iota(i32, (64, 128), 1)
    even = (lane & 7) < 4
    keep = (lane < 4) | (lane >= 124)
    even_x = lax.rem(lax.axis_index("gx"), 2) == 0
    even_y = lax.rem(lax.axis_index("gy"), 2) == 0
    rows = (own_0, own_1, got_0, got_1)
    for f in range(4):
        both = jnp.where(even == even_y, edge_0[f], edge_1[f])
        for r in range(16):
            ext[f, r, :, 0:128] = extended_row(rows, f, r, even_x)
            ext[f, r, :, 128:256] = jnp.where(keep, both if r == 0 else pltpu.roll(both, 128 - 8 * r, 1), 0.0)

    def faces(r, _):
        e = ext[0, r]
        wx[r] = face(e, ext[0, jnp.minimum(r + 1, 15)])
        wy[r] = face(e, up_y(e))
        wz[r] = face(e, up_z(e))
        return 0
    lax.fori_loop(0, 16, faces, 0)

    def sources(r, _):
        e = ext[0, r]
        y, z = wy[r], wz[r]
        d = SHIFT * e + wz[r] + down_z(z) + wx[r] + wx[r - 1] + y + down_y(y)
        outside = e == 0.0
        i = jnp.where(outside, 0.0, 1.0 / jnp.where(outside, 1.0, d))
        fy, fz = ext[2, r], ext[3, r]
        b = -0.5 * ((ext[1, r + 1] - ext[1, r - 1]) + (up_y(fy) - down_y(fy)) + (up_z(fz) - down_z(fz)))
        diag[r] = d
        inv[r] = i
        vs[0, r] = b * i
        return 0
    lax.fori_loop(1, 15, sources, 0)

    def spread(k, r):
        v = vs[k, r]
        y, z = wy[r], wz[r]
        total = wx[r] * vs[k, r + 1] + wx[r - 1] * vs[k, r - 1]
        total = total + y * up_y(v) + down_y(y * v)
        total = total + z * up_z(v) + down_z(z * v)
        return (diag[r] * v - total) * inv[r]

    for k, (lo, hi) in ((0, (2, 14)), (1, (3, 13))):
        def image(r, _, k=k):
            vs[k + 1, r] = spread(k, r)
            return 0
        lax.fori_loop(lo, hi, image, 0)

    def sums(r, total):
        d = diag[r][:, 0:128]
        v0, v1, v2 = (vs[k, r][:, 0:128] for k in range(3))
        v3 = spread(2, r)[:, 0:128]
        d0, d1, d2 = d * v0, d * v1, d * v2
        terms = (d0 * v0, d0 * v1, d1 * v1, d1 * v2, d2 * v2, d2 * v3)
        return tuple(t + jnp.sum(x.reshape(8, 8, 128), axis=0) for t, x in zip(total, terms))
    total = lax.fori_loop(4, 12, sums, tuple(jnp.zeros((8, 128), f32) for _ in range(6)))
    row = jnp.zeros((1, 128), f32)
    first = lax.broadcasted_iota(i32, (1, 128), 1)
    for k in range(6):
        row = jnp.where(first == k, jnp.sum(total[k]), row)
    moments[...] = jnp.broadcast_to(row[:, None, :], moments.shape)


def sweeps(rows, edge_0, edge_1):
    big = pltpu.VMEM((16, 64, 256), f32)
    return pl.pallas_call(
        sweeps_kernel,
        out_shape=(S((3, 16, 64, 256), f32), S((NGX * NGY, 1, 128), f32)),
        in_specs=[VSPEC] * 6,
        out_specs=(VSPEC,) * 2,
        scratch_shapes=[pltpu.VMEM((4, 16, 64, 256), f32)] + [big] * 7,
        compiler_params=VM,
        name="sweeps",
    )(*rows, edge_0, edge_1)


def coefficients(mu):
    def form(a, b, shift):
        return sum(a[i] * b[j] * mu[i + j + shift] for i in range(len(a)) for j in range(len(b)))
    zero = jnp.zeros_like(mu[0])
    one = jnp.ones_like(mu[0])
    pressure = [zero, zero, zero]
    scaled, direction = [one], [one]
    norm = mu[0]
    for sweep in range(3):
        step = norm / form(direction, direction, 1)
        for i, c in enumerate(direction):
            pressure[i] = pressure[i] + step * c
        if sweep < 2:
            moved = [zero] + direction
            old = scaled + [zero] * (len(moved) - len(scaled))
            scaled = [a - step * b for a, b in zip(old, moved)]
            following = form(scaled, scaled, 0)
            ratio = following / norm
            direction = [a + ratio * b for a, b in zip(scaled, direction + [zero])]
            norm = following
    return pressure


def gradient_kernel(all_moments, vs, pressure, table, p):
    summed = jnp.sum(all_moments[...], axis=0)
    mu = [jnp.broadcast_to(summed[:, k:k + 1], (8, 256)) for k in range(6)]
    coef = [jnp.broadcast_to(c[:1], (64, 256)) for c in coefficients(mu)]

    def combine(r, _):
        p[r] = coef[0] * vs[0, r] + coef[1] * vs[1, r] + coef[2] * vs[2, r]
        return 0
    lax.fori_loop(3, 13, combine, 0)
    for x in range(8):
        here = p[x + 4]
        core = here[:, 0:128]
        pressure[pl.ds(x, 64, stride=8), :] = core
        put_table(table, 0, x, 0.5 * (p[x + 5][:, 0:128] - p[x + 3][:, 0:128]))
        put_table(table, 1, x, 0.5 * (up_y(here) - down_y(here))[:, 0:128])
        put_table(table, 2, x, 0.5 * (up_z(core) - down_z(core)))


def gradients(all_moments, vs):
    return pl.pallas_call(
        gradient_kernel,
        out_shape=(S((512, 128), f32), S((NW, 48, 256), bf16)),
        in_specs=[VSPEC] * 2,
        out_specs=(VSPEC,) * 2,
        scratch_shapes=[pltpu.VMEM((16, 64, 256), f32)],
        compiler_params=VM,
        name="gradients",
    )(all_moments, vs)


def arrange_kernel(*refs):
    for i, out in enumerate(refs[3:]):
        for d in range(3):
            out[d * PR:(d + 1) * PR, :] = refs[d][i * PR:(i + 1) * PR, :]


def arrange(*arrays):
    return pl.pallas_call(
        arrange_kernel,
        out_shape=(S((3 * PR, 128), f32),) * 5,
        in_specs=[VSPEC] * 3,
        out_specs=(VSPEC,) * 5,
        compiler_params=VM,
        name="arrange",
    )(*arrays)


def place_kernel(back_refs, groups, *refs):
    n = back_refs
    backs, (pos_a, pos_b), out = refs[:n], refs[n:n + 2], refs[n + 2]
    stage, found, tiles, zeros, sem_zero, sem_tile = refs[n + 3:]
    hx, hy = lax.axis_index("gx"), lax.axis_index("gy")
    zeros[...] = jnp.zeros_like(zeros)

    def tile_at(t):
        return out.at[:, 0, pl.ds(pl.multiple_of(t * 8, 8), 8), :]

    def far(t):
        return jnp.abs(t - hx) > 2
    for t in range(16):
        @pl.when(far(t))
        def _():
            pltpu.make_async_copy(zeros, tile_at(t), sem_zero.at[t]).start()
    where = {-2: 0, -1: 1, 0: 2, 1: 3, 2: 4}
    for g, runs in enumerate(groups):
        side = lax.rem(hx // abs(runs[0][0]), 2) == 0
        pair = (backs[0], backs[1]) if g == 0 else (backs[3], backs[4])
        up = lax.rem(hy, 2) == 0
        sources = (jnp.where(up, 2 * PR, 0), PR, jnp.where(up, 0, 2 * PR))
        for ref, first in zip(pair, (jnp.where(side, 3 * PR, 0), jnp.where(side, 0, 3 * PR))):
            for d in range(3):
                to = pl.multiple_of(first + d * PR, 8)
                stage[pl.ds(to, PR), :] = ref[pl.ds(pl.multiple_of(sources[d], 8), PR), :]
        _, dy0, first, count = runs[2]
        for d in range(count):
            src = pl.multiple_of(sources[dy0 + 1 + d], 8)
            stage[(first + d) * PR:(first + d + 1) * PR, :] = backs[2][pl.ds(src, PR), :]
        if g == 1:
            stage[7 * PR:8 * PR, :] = jnp.zeros((PR, 128), f32)
        pos_ref = (pos_a, pos_b)[g]

        def chunk(c, _):
            k = pos_ref[c]
            at, src = k & 127, k >> 7
            acc = [jnp.zeros((8, 128), f32) for _ in range(3)]
            for v in range(CH):
                here = src == v
                for f in range(3):
                    got = jnp.take_along_axis(stage[pl.ds(f * CH + v, 8, stride=PR), :], at, axis=1)
                    acc[f] = jnp.where(here, got, acc[f])
            for f in range(3):
                found[g, f, c] = acc[f]
            return 0
        lax.fori_loop(0, CH, chunk, 0)
    row = lax.broadcasted_iota(i32, (8, 128), 0)
    for dx in (-2, -1, 0, 1, 2):
        pieces = [(g, run) for g, runs in enumerate(groups) for run in runs if run[0] == dx]
        turned = []
        for g, (_, dy0, first, count) in pieces:
            shift = lax.rem(hy + dy0 - first + 16, 8)
            low = hy + dy0
            turned.append((g, shift, (row >= low) & (row < low + count)))
        for f in range(3):
            for c in range(CH):
                got = jnp.zeros((8, 128), f32)
                for g, shift, mask in turned:
                    got = jnp.where(mask, pltpu.roll(found[g, f, c], shift, 0), got)
                tiles[where[dx], f, :, c * 128:(c + 1) * 128] = got

        @pl.when((hx + dx >= 0) & (hx + dx < NGX))
        def _():
            pltpu.make_async_copy(tiles.at[where[dx]], tile_at(hx + dx), sem_tile.at[where[dx]]).start()
    for t in range(16):
        @pl.when(far(t))
        def _():
            pltpu.make_async_copy(zeros, tile_at(t), sem_zero.at[t]).wait()
    for dx in (-2, -1, 0, 1, 2):
        @pl.when((hx + dx >= 0) & (hx + dx < NGX))
        def _():
            pltpu.make_async_copy(tiles.at[where[dx]], tile_at(hx + dx), sem_tile.at[where[dx]]).wait()


def place_forces(backs, pos):
    return pl.pallas_call(
        functools.partial(place_kernel, len(backs), GROUPS),
        out_shape=S((3, 1, 128, 3072), f32),
        in_specs=[VSPEC] * (len(backs) + 2),
        out_specs=pl.BlockSpec(memory_space=pl.ANY),
        scratch_shapes=[
            pltpu.VMEM((8 * PR, 128), f32),
            pltpu.VMEM((2, 3, CH, 8, 128), f32),
            pltpu.VMEM((5, 3, 8, 3072), f32),
            pltpu.VMEM((3, 8, 3072), f32),
            pltpu.SemaphoreType.DMA((16,)),
            pltpu.SemaphoreType.DMA((5,)),
        ],
        compiler_params=VM,
        name="place_forces",
    )(*backs, *pos)


def exchange(x, axis, by, which):
    count = {"gx": NGX, "gy": NGY}[axis]
    pairs = [(i, i + by) for i in range(count - by) if (i // by) % 2 == which]
    return lax.ppermute(x, axis, pairs + [(j, i) for i, j in pairs])


def per_device(particle_data, particle_cells, slot_counts, fluid_velocity):
    two_0, two_1, zero_a, keys_a = sort_blocks(GROUPS[0], particle_data, particle_cells, slot_counts)
    two_0, two_1 = exchange(two_0, "gx", 2, 0), exchange(two_1, "gx", 2, 1)
    one_0, one_1, zero_b, keys_b = sort_blocks(GROUPS[1], particle_data, particle_cells, slot_counts)
    one_0, one_1 = exchange(one_0, "gx", 1, 0), exchange(one_1, "gx", 1, 1)
    along = [two_0, two_1, jnp.concatenate([zero_a, zero_b], axis=0), one_0, one_1]
    below, mine, above = [jnp.concatenate([a[d * BR:(d + 1) * BR] for a in along], axis=0) for d in range(3)]
    up = lax.rem(lax.axis_index("gy"), 2) == 0
    sides = [
        exchange(jnp.where(up, above, below), "gy", 1, 0),
        exchange(jnp.where(up, below, above), "gy", 1, 1),
    ]
    bases = tuple(range(0, 5 * BR, BR))
    acc = deposit([mine], bases, 8)
    table, own_0, own_1, token = deposit(sides, bases, 4, acc, fluid_velocity.reshape(3, 512, 128))
    rows = (own_0, own_1, exchange(own_0, "gx", 1, 0), exchange(own_1, "gx", 1, 1))
    *pos, token = inverse(keys_a, keys_b, token)
    packed = pack_edges(rows, token)
    vs, moments = sweeps(rows, exchange(packed, "gy", 1, 0), exchange(packed, "gy", 1, 1))
    everyone = lax.all_to_all(moments, ("gx", "gy"), 0, 0)
    pressure, slopes = gradients(everyone, vs)
    far_0, far_1, token = interp(sides, bases, table, slopes, 4, token, 2)
    back = [exchange(far_0, "gy", 1, 0), exchange(far_1, "gy", 1, 1)]
    near, _ = interp([mine], bases, table, slopes, 8, token, 1)
    blocks = list(arrange(back[0], near, back[1]))
    for i, (by, which) in ((0, (2, 0)), (1, (2, 1)), (3, (1, 0)), (4, (1, 1))):
        blocks[i] = exchange(blocks[i], "gx", by, which)
    drag = place_forces(blocks, pos)
    return pressure.reshape(64, 8, 128), drag


def solution(mesh):
    return jax.shard_map(
        per_device,
        mesh=mesh,
        in_specs=(
            P(None, ("gx", "gy"), None, None),
            P(None, ("gx", "gy"), None, None),
            P(("gx", "gy"), None),
            P(None, None, "gx", "gy"),
        ),
        out_specs=(P(None, "gx", "gy"), P(None, ("gx", "gy"), None, None)),
        check_vma=False,
    )
```

```python
import functools
import jax
import jax.numpy as jnp
from jax import lax
from jax.experimental import pallas as pl
from jax.experimental.pallas import tpu as pltpu
from jax.sharding import PartitionSpec as P

f32, bf16, i32 = jnp.float32, jnp.bfloat16, jnp.int32
CH = 24
BR = 152
WL = 16
NW = 32
SPAN = WL * 128
PR = 3 * CH
VM = pltpu.CompilerParams(vmem_limit_bytes=56 * 1024 * 1024)
VSPEC = pl.BlockSpec(memory_space=pltpu.VMEM)
S = jax.ShapeDtypeStruct
TOKEN = S((8, 128), f32)


def sort_network(x):
    lane = lax.broadcasted_iota(i32, (1, 8, 128), 2)
    flipped = None
    for merge in range(1, 13):
        if merge < 12:
            if merge >= 5:
                want = (lane >> (merge - 5)) & 1
                mask = -want
            else:
                mask = jnp.asarray(-((lax.broadcasted_iota(i32, (32, 8, 128), 0) >> merge) & 1))
        else:
            mask = None
        if mask is not None:
            x = x ^ mask
        for bit in range(merge - 1, -1, -1):
            if bit < 5:
                step = 1 << bit
                y = x.reshape(32 // (2 * step), 2, step, 8, 128)
                a, b = y[:, 0], y[:, 1]
                x = jnp.stack([jnp.minimum(a, b), jnp.maximum(a, b)], axis=1).reshape(32, 8, 128)
            else:
                step = 1 << (bit - 5)
                up = (lane & step) != 0
                other = jnp.take_along_axis(x, jnp.broadcast_to(lane ^ step, x.shape), axis=2)
                x = jnp.where(up, jnp.maximum(x, other), jnp.minimum(x, other))
        if mask is not None:
            x = x ^ mask
    return x


def lanes_to_chunks(x):
    lane = lax.broadcasted_iota(i32, (1, 8, 128), 2)
    for bit in range(5):
        step = 1 << bit
        y = x.reshape(32 // (2 * step), 2, step, 8, 128)
        a, b = y[:, 0], y[:, 1]
        up = ((lane & step) != 0)[:, None]
        na = jnp.where(up, pltpu.roll(b, step, 3), a)
        nb = jnp.where(up, b, pltpu.roll(a, 128 - step, 3))
        x = jnp.stack([na, nb], axis=1).reshape(32, 8, 128)
    for bit in range(2):
        step, far = 1 << bit, 32 << bit
        y = x.reshape(32 // (2 * step), 2, step, 8, 128)
        a, b = y[:, 0], y[:, 1]
        up = ((lane & far) != 0)[:, None]
        na = jnp.where(up, pltpu.roll(b, far, 3), a)
        nb = jnp.where(up, b, pltpu.roll(a, 128 - far, 3))
        x = jnp.stack([na, nb], axis=1).reshape(32, 8, 128)
    return jnp.stack([x[(c % 8) * 4 + c // 8] for c in range(32)], axis=0)


GROUPS = (((-2, -1, 0, 3), (2, -1, 3, 3), (0, -1, 6, 2)), ((-1, -1, 0, 3), (1, -1, 3, 3), (0, 1, 6, 1)))
NGX, NGY = 16, 8


def unrolled(count, by, body):
    def several(i, _):
        for j in range(by):
            body(i * by + j)
        return 0
    lax.fori_loop(0, count // by, several, 0)


def row_mask(first, count):
    row = lax.broadcasted_iota(i32, (8, 128), 0)
    return (row >= first) & (row < first + count)


def sort_kernel(runs, n_out, data_ref, cells_ref, counts_ref, *rest):
    outs, pos_ref = rest[:n_out], rest[n_out]
    data_v, cells_v, key_s, pay_s, out_s, sems = rest[n_out + 1:]
    hx, hy = lax.axis_index("gx"), lax.axis_index("gy")
    copies = []
    for t, (dx, _, _, _) in enumerate(runs):
        tile = pl.ds(pl.multiple_of(jnp.clip(hx + dx, 0, NGX - 1) * 8, 8), 8)
        copies.append(pltpu.make_async_copy(cells_ref.at[:, 0, tile, :], cells_v.at[t], sems.at[2 * t]))
    for t, (dx, _, _, _) in enumerate(runs):
        tile = pl.ds(pl.multiple_of(jnp.clip(hx + dx, 0, NGX - 1) * 8, 8), 8)
        copies.append(pltpu.make_async_copy(data_ref.at[:, 0, tile, :], data_v.at[t], sems.at[2 * t + 1]))
    for copy in copies:
        copy.start()
    lane = lax.broadcasted_iota(i32, (8, 128), 1)
    row = lax.broadcasted_iota(i32, (8, 128), 0)
    counts = jnp.zeros((8, 128), i32)
    for dx, dy0, first, count in runs:
        for i in range(count):
            bx, by = hx + dx, hy + dy0 + i
            valid = (bx >= 0) & (bx < NGX) & (by >= 0) & (by < NGY)
            n = counts_ref[0, jnp.clip(bx * NGY + by, 0, NGX * NGY - 1)]
            counts = jnp.where(row == first + i, jnp.where(valid, n, 0), counts)
    shifts = [lax.rem(first - (hy + dy0) + 16, 8) for _, dy0, first, _ in runs]
    masks = [row_mask(first, count) for _, _, first, count in runs]
    for copy in copies[:len(runs)]:
        copy.wait()

    def gathered(ref, f, c):
        got = None
        for t in range(len(runs)):
            x = pltpu.roll(ref[t, f, :, c * 128:(c + 1) * 128], shifts[t], 0)
            got = x if got is None else jnp.where(masks[t], x, got)
        return got

    rows = []
    for c in range(32):
        slot = lane + c * 128
        if c < CH:
            h, col = gathered(cells_v, 0, c), gathered(cells_v, 1, c)
            live = slot < counts
            cell = (((col >> 7) * 64 + h) << 7) + (col & 127)
            cell = jnp.where(live, cell, 65536)
            rows.append((cell << 12) + slot)
        else:
            rows.append((1 << 29) + slot)
    keys = lanes_to_chunks(sort_network(jnp.stack(rows, axis=0)))
    key_s[...] = keys[:CH]
    pos_ref[...] = keys[:CH]
    for copy in copies[len(runs):]:
        copy.wait()
    for c in range(CH):
        for f in range(5):
            pay_s[f, c] = jnp.where(lane + c * 128 < counts, gathered(data_v, f, c), 0.0)

    def chunk(c):
        k = key_s[c]
        slot = k & 4095
        at, src = slot & 127, slot >> 7
        acc = [jnp.zeros((8, 128), f32) for _ in range(5)]
        for v in range(CH):
            here = src == v
            for f in range(5):
                got = jnp.take_along_axis(pay_s[f, v], at, axis=1)
                acc[f] = jnp.where(here, got, acc[f])
        for f in range(5):
            out_s[pl.ds(f * CH + c, 8, stride=BR), :] = acc[f]
        out_s[pl.ds(5 * CH + c, 8, stride=BR), :] = (k >> 12).astype(f32)
    unrolled(CH, 4, chunk)
    low = lane < 64
    bound = jnp.where(low, lane, lane - 63) * SPAN
    total = jnp.zeros((8, 128), i32)
    for c in range(CH):
        cell = key_s[c] >> 12
        last = jnp.broadcast_to(cell[:, 127:128], (8, 128))
        start = jnp.broadcast_to(cell[:, 0:1], (8, 128))
        total = total + jnp.where(jnp.where(low, last, start) < bound, 1, 0)
    for r in range(8):
        out_s[pl.ds(6 * CH + r, 8, stride=BR), :] = total.astype(f32)
    side = lax.rem(hx // abs(runs[0][0]), 2) == 0
    for out, first in ((outs[0], jnp.where(side, 3 * BR, 0)), (outs[1], jnp.where(side, 0, 3 * BR))):
        out[...] = out_s[pl.ds(pl.multiple_of(first, 8), 3 * BR), :]
    _, _, first, count = runs[2]
    outs[2][...] = out_s[first * BR:(first + count) * BR, :]


def inverse_kernel(keys_a, keys_b, after, pos_a, pos_b, token):
    token[...] = after[...]
    place = lax.broadcasted_iota(i32, (CH, 8, 128), 0) * 128 + lax.broadcasted_iota(i32, (CH, 8, 128), 2)
    rest = jnp.full((32 - CH, 8, 128), 1 << 29, i32)
    for keys, pos in ((keys_a, pos_a), (keys_b, pos_b)):
        back = jnp.concatenate([((keys[...] & 4095) << 12) + place, rest], axis=0)
        pos[...] = lanes_to_chunks(sort_network(back))[:CH] & 4095


def inverse(keys_a, keys_b, after):
    shape = jax.ShapeDtypeStruct((CH, 8, 128), i32)
    return pl.pallas_call(
        inverse_kernel,
        out_shape=(shape, shape, TOKEN),
        in_specs=[VSPEC] * 3,
        out_specs=(VSPEC,) * 3,
        compiler_params=VM,
        cost_estimate=pl.CostEstimate(flops=10**9, bytes_accessed=2 * 10**7, transcendentals=0),
        name="inverse",
    )(keys_a, keys_b, after)


def sort_blocks(runs, data, cells, counts):
    shapes = [jax.ShapeDtypeStruct((count * BR, 128), f32) for _, _, _, count in runs]
    shapes.append(jax.ShapeDtypeStruct((CH, 8, 128), i32))
    n = len(runs)
    return pl.pallas_call(
        functools.partial(sort_kernel, runs, n),
        out_shape=tuple(shapes),
        in_specs=[pl.BlockSpec(memory_space=pl.ANY)] * 2 + [pl.BlockSpec(memory_space=pltpu.SMEM)],
        out_specs=(pl.BlockSpec(memory_space=pltpu.VMEM),) * (n + 1),
        scratch_shapes=[
            pltpu.VMEM((n, 5, 8, 3072), f32),
            pltpu.VMEM((n, 2, 8, 3072), i32),
            pltpu.VMEM((CH, 8, 128), i32),
            pltpu.VMEM((5, CH, 8, 128), f32),
            pltpu.VMEM((8 * BR, 128), f32),
            pltpu.SemaphoreType.DMA((2 * n,)),
        ],
        compiler_params=VM,
        name="sort_blocks",
    )(data, cells, counts)


def load_offsets(refs, off_v, off_s, sem):
    for j, (ref, base) in enumerate(refs):
        off_v[j:j + 1, :] = ref[base + 6 * CH:base + 6 * CH + 1, :].astype(i32)
    copy = pltpu.make_async_copy(off_v, off_s, sem)
    copy.start()
    copy.wait()


def wide(row, rows):
    return jnp.broadcast_to(row, (rows, 128))


def split_cell(cell):
    line = jnp.floor(cell * (1.0 / 128.0))
    return line, cell - line * 128.0


def width_onehot(wid, iota):
    w16 = wide(wid, 16).astype(bf16)
    w = jnp.concatenate([w16] * 8, axis=0)
    return jnp.where(w == iota, jnp.asarray(1.0, bf16), jnp.asarray(0.0, bf16))


def deposit_kernel(nref, bases, unroll, use_acc, *refs):
    blocks = [(refs[i], b) for i in range(nref) for b in bases]
    nb = len(blocks)
    rest = refs[nref:]
    if use_acc:
        prev, fluid, table, own, send_0, send_1, token, out, flux, pre, off_v, off_s, sem = rest
    else:
        out, pre, off_v, off_s, sem = rest
    load_offsets(blocks, off_v, off_s, sem)
    for j, (ref, base) in enumerate(blocks):
        vol = ref[base:base + CH, :]
        coef = ref[base + CH:base + 2 * CH, :]
        vals = [vol, coef] + [coef * ref[base + (2 + d) * CH:base + (3 + d) * CH, :] for d in range(3)]
        for k, v in enumerate(vals):
            hi = v.astype(bf16).astype(f32)
            pre[j, k] = hi
            pre[j, 5 + k] = v - hi
        line, wid = split_cell(ref[base + 5 * CH:base + 6 * CH, :])
        pre[j, 10] = line
        pre[j, 11] = wid
    iota = lax.broadcasted_iota(i32, (128, 128), 0).astype(f32).astype(bf16)
    iota16 = lax.broadcasted_iota(i32, (16, 128), 0).astype(f32).astype(bf16)
    zero = jnp.zeros((16, 128), bf16)

    def operands(j, c, w):
        rel = jnp.clip(pre[j, 10, pl.ds(c, 1), :] - (w * WL).astype(f32), -1.0, 16.0)
        mask = wide(rel, 16).astype(bf16) == iota16
        a = jnp.concatenate(
            [jnp.where(mask, wide(pre[j, k, pl.ds(c, 1), :], 16).astype(bf16), zero) for k in range(10)], axis=0)
        return a, width_onehot(pre[j, 11, pl.ds(c, 1), :], iota)

    def product(a, b):
        p = lax.dot_general(a, b, (((1,), (1,)), ((), ())), preferred_element_type=f32)
        return p

    def halves(p):
        return (p[:80] + p[80:]).reshape(5, WL, 128)

    def windows(i, more):
        for u in range(unroll):
            w = i * unroll + u
            total = None
            for j in range(nb):
                first = jnp.minimum(off_s[j, w], CH - 2)
                more = jnp.maximum(more, off_s[j, 64 + w] - first)
                a0, b0 = operands(j, first, w)
                a1, b1 = operands(j, first + 1, w)
                p = product(jnp.concatenate([a0, a1], axis=1), jnp.concatenate([b0, b1], axis=1))
                total = p if total is None else total + p
            total = halves(total)
            rows = pl.ds(pl.multiple_of(w * WL, WL), WL)
            if use_acc:
                total = total + prev[:, rows, :]
            out[:, rows, :] = total
        return more
    more = lax.fori_loop(0, NW // unroll, windows, jnp.int32(0))

    @pl.when(more > 2)
    def _():
        def window(w, _):
            rows = pl.ds(pl.multiple_of(w * WL, WL), WL)

            def block(j, _):
                def step(c, _):
                    a, b = operands(j, c, w)
                    out[:, rows, :] += halves(product(a, b))
                    return 0
                return lax.fori_loop(jnp.minimum(off_s[j, w], CH - 2) + 2, off_s[j, 64 + w], step, 0)
            return lax.fori_loop(0, nb, block, 0)
        lax.fori_loop(0, NW, window, 0)


    if use_acc:
        fields(out, fluid, table, own, send_0, send_1, flux)
        token[...] = jnp.zeros_like(token)


def deposit(arrays, bases, unroll, prev=None, fluid=None):
    nb = len(arrays) * len(bases)
    args = list(arrays) + ([] if prev is None else [prev, fluid])
    total = S((5, 512, 128), f32)
    sent = S((SENT, 64, 128), f32)
    shapes = (S((NW, 48, 256), bf16), S((2, 8, 64, 128), f32), sent, sent, TOKEN)
    scratch = [
        pltpu.VMEM((nb, 12, CH, 128), f32),
        pltpu.VMEM((nb, 128), i32),
        pltpu.SMEM((nb, 128), i32),
        pltpu.SemaphoreType.DMA,
    ]
    if prev is not None:
        scratch = [pltpu.VMEM((5, 512, 128), f32), pltpu.VMEM((8, 64, 128), f32)] + scratch
    return pl.pallas_call(
        functools.partial(deposit_kernel, len(arrays), bases, unroll, prev is not None),
        out_shape=total if prev is None else shapes,
        in_specs=[VSPEC] * len(args),
        out_specs=VSPEC if prev is None else (VSPEC,) * 5,
        scratch_shapes=scratch,
        compiler_params=VM,
        cost_estimate=pl.CostEstimate(flops=10**9 * nb, bytes_accessed=3 * 10**6 * nb, transcendentals=0),
        name="deposit",
    )(*args)


def interp_kernel(nref, bases, unroll, *refs):
    blocks = [(refs[i], b) for i in range(nref) for b in bases]
    nb = len(blocks)
    fast, slope, _ = refs[nref:nref + 3]
    outs = refs[nref + 3:-6]
    token, pre, acc, off_v, off_s, sem = refs[-6:]
    each = nb // len(outs)
    token[...] = jnp.zeros_like(token)
    load_offsets(blocks, off_v, off_s, sem)
    for j, (ref, base) in enumerate(blocks):
        line, wid = split_cell(ref[base + 5 * CH:base + 6 * CH, :])
        pre[j, 0] = line
        pre[j, 1] = wid
        pre[j, 2] = ref[base + CH:base + 2 * CH, :]
        pre[j, 3] = -ref[base:base + CH, :]
    acc[...] = jnp.zeros_like(acc)
    iota = lax.broadcasted_iota(i32, (128, 128), 0).astype(f32).astype(bf16)
    iota16 = lax.broadcasted_iota(i32, (16, 128), 0).astype(f32)

    def visit(j, c, w, width, tab):
        scales, hots = [], []
        for i in range(width):
            at = pl.ds(c + i, 1)
            mask = wide(pre[j, 0, at, :] - (w * WL).astype(f32), 16) == iota16
            scales.append([jnp.where(mask, wide(pre[j, 2 + s, at, :], 16), 0.0) for s in range(2)])
            b = width_onehot(pre[j, 1, at, :], iota)
            hots.append(jnp.concatenate([b, b], axis=0))
        hot = hots[0] if width == 1 else jnp.concatenate(hots, axis=1)
        g = jnp.dot(tab, hot, preferred_element_type=f32)
        for i in range(width):
            for k in range(3):
                lanes = slice(i * 128, (i + 1) * 128)
                part = scales[i][0] * g[k * 16:k * 16 + 16, lanes]
                part = part + scales[i][1] * g[48 + k * 16:64 + k * 16, lanes]
                acc[j, c + i, k] += part[:8] + part[8:]

    def windows(i, more):
        for u in range(unroll):
            w = i * unroll + u
            tab = jnp.concatenate([fast[w], slope[w]], axis=0)
            for j in range(nb):
                first = jnp.minimum(off_s[j, w], CH - 2)
                more = jnp.maximum(more, off_s[j, 64 + w] - first)
                visit(j, first, w, 2, tab)
        return more
    more = lax.fori_loop(0, NW // unroll, windows, jnp.int32(0))

    @pl.when(more > 2)
    def _():
        def window(w, _):
            tab = jnp.concatenate([fast[w], slope[w]], axis=0)

            def block(j, _):
                def step(c, _):
                    visit(j, c, w, 1, tab)
                    return 0
                return lax.fori_loop(jnp.minimum(off_s[j, w], CH - 2) + 2, off_s[j, 64 + w], step, 0)
            return lax.fori_loop(0, nb, block, 0)
        lax.fori_loop(0, NW, window, 0)
    for j, (ref, base) in enumerate(blocks):
        coef = ref[base + CH:base + 2 * CH, :]
        for k in range(3):
            vel = ref[base + (2 + k) * CH:base + (3 + k) * CH, :]
            at = (j % each) * PR + k * CH
            outs[j // each][at:at + CH, :] = jnp.sum(acc[j, :, k], axis=1) - coef * vel


def interp(arrays, bases, fast, slope, unroll, after, n_out):
    nb = len(arrays) * len(bases)
    args = list(arrays) + [fast, slope, after]
    return pl.pallas_call(
        functools.partial(interp_kernel, len(arrays), bases, unroll),
        out_shape=(S((nb // n_out * PR, 128), f32),) * n_out + (TOKEN,),
        in_specs=[VSPEC] * len(args),
        out_specs=(VSPEC,) * (n_out + 1),
        scratch_shapes=[
            pltpu.VMEM((nb, 4, CH, 128), f32),
            pltpu.VMEM((nb, CH, 3, 8, 128), f32),
            pltpu.VMEM((nb, 128), i32),
            pltpu.SMEM((nb, 128), i32),
            pltpu.SemaphoreType.DMA,
        ],
        compiler_params=VM,
        cost_estimate=pl.CostEstimate(flops=10**9 * nb, bytes_accessed=3 * 10**6 * nb, transcendentals=0),
        name="interp",
    )(*args)

TIME_STEP = 0.1
SHIFT = 0.05


def put_table(table, k, x, values):
    hi = values.astype(bf16)
    lo = (values - hi.astype(f32)).astype(bf16)
    for q in range(4):
        table[4 * x + q, k * 16:k * 16 + 16, 0:128] = hi[16 * q:16 * q + 16]
        table[4 * x + q, k * 16:k * 16 + 16, 128:256] = lo[16 * q:16 * q + 16]


def up_z(x):
    return jnp.concatenate([x[1:], jnp.zeros_like(x[:1])], axis=0)


def down_z(x):
    return jnp.concatenate([jnp.zeros_like(x[:1]), x[:-1]], axis=0)


def plane_lanes():
    return lax.broadcasted_iota(i32, (64, 128), 1)


def is_even(axis):
    return lax.rem(lax.axis_index(axis), 2) == 0


def turn(x, by):
    return x if by % 128 == 0 else pltpu.roll(x, by % 128, 1)


SENT = 9


def fields(acc, fluid, table, own, send_0, send_1, flux):
    even = is_even("gx")
    lane = plane_lanes()
    ends = jnp.zeros((64, 128), f32)
    for x in range(8):
        at = slice(x * 64, x * 64 + 64)
        fraction = acc[0, at, :]
        drag = acc[1, at, :]
        porosity = 1.0 / (1.0 + fraction)
        fluxes = []
        for d in range(3):
            fluid_d = fluid[d, pl.ds(x, 64, stride=8), :]
            predicted = fluid_d + TIME_STEP * (1.0 + fraction) * (acc[2 + d, at, :] - drag * fluid_d)
            put_table(table, d, x, predicted)
            fluxes.append(porosity * predicted)
        flux[x] = fluxes[0]
        fy, fz = fluxes[1:]
        along_y = jnp.where(lane < 127, turn(fy, -1), 0.0) - jnp.where(lane > 0, turn(fy, 1), 0.0)
        own[0, x] = porosity
        own[1, x] = -0.5 * (along_y + (up_z(fz) - down_z(fz)))
        mid = 8 * (x + 4)
        ends = jnp.where((lane == mid) | (lane == mid - 1), turn(fy, mid), ends)
    for x in range(8):
        along_x = (flux[x + 1] if x < 7 else 0.0) - (flux[x - 1] if x > 0 else 0.0)
        own[1, x] = own[1, x] - 0.5 * along_x
    low = [own[0, x] for x in range(4)] + [own[1, x] for x in range(3)] + [flux[0], ends]
    high = [own[0, x] for x in range(4, 8)] + [own[1, x] for x in range(5, 8)] + [flux[7], ends]
    for i in range(SENT):
        send_0[i] = jnp.where(even, high[i], low[i])
        send_1[i] = jnp.where(even, low[i], high[i])


def extended(refs):
    own, sent_0, sent_1, got_0, got_1 = refs
    even = is_even("gx")

    def below(i):
        return jnp.where(even, got_1[i], got_0[i])

    def above(i):
        return jnp.where(even, got_0[i], got_1[i])

    def porosity(r):
        return below(r) if r < 4 else own[0, r - 4] if r < 12 else above(r - 12)

    def source(r):
        if r == 3:
            return below(6) - 0.5 * jnp.where(even, sent_1[7], sent_0[7])
        if r == 4:
            return own[1, 0] + 0.5 * below(7)
        if r == 11:
            return own[1, 7] - 0.5 * above(7)
        if r == 12:
            return above(4) + 0.5 * jnp.where(even, sent_0[7], sent_1[7])
        return below(3 + r) if r < 4 else own[1, r - 4] if r < 12 else above(r - 8)

    def ends():
        lane = plane_lanes()
        beside = jnp.where((lane >= 92) & (lane < 124), turn(above(8), 64), turn(below(8), 64))
        return jnp.where((lane >= 28) & (lane < 92), sent_0[8], beside)
    return porosity, source, ends


def pack_kernel(own, sent_0, sent_1, got_0, got_1, after, out):
    del after
    porosity, source, ends = extended((own, sent_0, sent_1, got_0, got_1))
    lane = plane_lanes()
    for f, (rows, get) in enumerate(((range(16), porosity), (range(1, 15), source))):
        got = jnp.zeros((64, 128), f32)
        for r in rows:
            place = (lax.rem(lane + 132 - 8 * r, 128)) < 8
            got = jnp.where(place, turn(get(r), 8 * r), got)
        out[f] = got
    out[2] = ends()


def pack_edges(refs, after):
    return pl.pallas_call(
        pack_kernel,
        out_shape=S((3, 64, 128), f32),
        in_specs=[VSPEC] * 6,
        out_specs=VSPEC,
        compiler_params=VM,
        name="pack_edges",
    )(*refs, after)


def face(e, n):
    return 2.0 * e * n / jnp.maximum(e + n, 1e-30)


def up_pair(pair, last):
    a, b = (pltpu.roll(x, 127, 1) for x in pair)
    return jnp.where(last, b, a), jnp.where(last, a, b)


def down_pair(pair, first):
    a, b = (pltpu.roll(x, 1, 1) for x in pair)
    return jnp.where(first, b, a), jnp.where(first, a, b)


MID, UP, DOWN = pl.ds(8, 64), pl.ds(9, 64), pl.ds(7, 64)


def sweeps_kernel(own, sent_0, sent_1, got_0, got_1, packed, edge_0, edge_1, core, beside, moments, vs, por, src, wx, wy, wz,
                  diag, inv):
    porosity, source, _ = extended((own, sent_0, sent_1, got_0, got_1))
    lane = plane_lanes()
    first, last = lane == 0, lane == 127
    keep = (lane < 4) | (lane >= 124)
    even_y = is_even("gy")

    def above(f):
        return jnp.where(even_y, edge_0[f], edge_1[f])

    def below(f):
        return jnp.where(even_y, edge_1[f], edge_0[f])
    part = lane & 7

    def crossed(from_below, from_above):
        return jnp.where(part == 0, 0.5 * turn(from_below, 1), jnp.where(part == 7, -0.5 * turn(from_above, -1), 0.0))
    side_e = jnp.where(part < 4, above(0), below(0))
    side_b = jnp.where(part < 4, above(1), below(1)) + crossed(packed[2], packed[2])
    core_b = crossed(below(2), above(2))
    for ref in (por, wz):
        for h in range(2):
            for r in range(16):
                ref[h, r, 0:8] = jnp.zeros((8, 128), f32)
                ref[h, r, 72:80] = jnp.zeros((8, 128), f32)
    for k in range(3):
        for r in range(1, 15):
            for h in range(2):
                vs[k, h, r, 0:8] = jnp.zeros((8, 128), f32)
                vs[k, h, r, 72:80] = jnp.zeros((8, 128), f32)
    for r in range(16):
        por[0, r, MID] = porosity(r)
        por[1, r, MID] = jnp.where(keep, turn(side_e, -8 * r), 0.0)
        if 0 < r < 15:
            src[0, r] = source(r) + jnp.where(first | last, turn(core_b, -8 * r), 0.0)
            src[1, r] = jnp.where(keep, turn(side_b, -8 * r), 0.0)

    def faces(r):
        pair = [por[h, r, MID] for h in range(2)]
        up = up_pair(pair, last)
        for h in range(2):
            wx[h, r] = face(pair[h], por[h, r + 1, MID])
            wy[h, r] = face(pair[h], up[h])
            wz[h, r, MID] = face(pair[h], por[h, r, UP])
    for r in range(15):
        faces(r)

    def keep_plane(k, h, r, v):
        vs[k, h, r, MID] = v
        if h == 0 and 3 <= r < 13:
            core[k, r - 3] = v
        if h == 1 and 4 <= r < 12:
            beside[k, r - 4] = v

    def sources(r):
        y = [wy[h, r] for h in range(2)]
        y_down = down_pair(y, first)
        for h in range(2):
            e = por[h, r, MID]
            d = SHIFT * e + wx[h, r] + wx[h, r - 1] + y[h] + y_down[h] + wz[h, r, MID] + wz[h, r, DOWN]
            outside = e == 0.0
            i = jnp.where(outside, 0.0, 1.0 / jnp.where(outside, 1.0, d))
            diag[h, r] = d
            inv[h, r] = i
            keep_plane(0, h, r, src[h, r] * i)
    for r in range(1, 15):
        sources(r)

    def spread(k, r, halves):
        pair = [vs[k, h, r, MID] for h in range(2)]
        y = [wy[h, r] for h in range(2)]
        up = up_pair(pair, last)
        down = down_pair([a * b for a, b in zip(y, pair)], first)
        made = []
        for h in range(halves):
            total = wx[h, r] * vs[k, h, r + 1, MID] + wx[h, r - 1] * vs[k, h, r - 1, MID]
            total = total + y[h] * up[h] + down[h]
            total = total + wz[h, r, MID] * vs[k, h, r, UP] + wz[h, r, DOWN] * vs[k, h, r, DOWN]
            made.append((diag[h, r] * pair[h] - total) * inv[h, r])
        return made

    for k, (lo, hi) in ((0, (2, 14)), (1, (3, 13))):
        for r in range(lo, hi):
            for h, v in enumerate(spread(k, r, 2)):
                keep_plane(k + 1, h, r, v)

    def sums(r, total):
        d = diag[0, r]
        v0, v1, v2 = (vs[k, 0, r, MID] for k in range(3))
        v3, = spread(2, r, 1)
        d0, d1, d2 = d * v0, d * v1, d * v2
        terms = (d0 * v0, d0 * v1, d1 * v1, d1 * v2, d2 * v2, d2 * v3)
        return tuple(t + jnp.sum(x.reshape(8, 8, 128), axis=0) for t, x in zip(total, terms))
    total = tuple(jnp.zeros((8, 128), f32) for _ in range(6))
    for r in range(4, 12):
        total = sums(r, total)
    row = jnp.zeros((1, 128), f32)
    place = lax.broadcasted_iota(i32, (1, 128), 1)
    for k in range(6):
        row = jnp.where(place == k, jnp.sum(total[k]), row)
    moments[...] = jnp.broadcast_to(row[:, None, :], moments.shape)


def sweeps(refs, packed, edge_0, edge_1):
    padded, plane = pltpu.VMEM((2, 16, 80, 128), f32), pltpu.VMEM((2, 16, 64, 128), f32)
    return pl.pallas_call(
        sweeps_kernel,
        out_shape=(S((3, 10, 64, 128), f32), S((3, 8, 64, 128), f32), S((NGX * NGY, 1, 128), f32)),
        in_specs=[VSPEC] * 8,
        out_specs=(VSPEC,) * 3,
        scratch_shapes=[pltpu.VMEM((3, 2, 16, 80, 128), f32), padded, plane, plane, plane, padded, plane, plane],
        compiler_params=VM,
        name="sweeps",
    )(*refs, packed, edge_0, edge_1)


def coefficients(mu):
    def form(a, b, shift):
        return sum(a[i] * b[j] * mu[i + j + shift] for i in range(len(a)) for j in range(len(b)))
    zero = jnp.zeros_like(mu[0])
    one = jnp.ones_like(mu[0])
    pressure = [zero, zero, zero]
    scaled, direction = [one], [one]
    norm = mu[0]
    for sweep in range(3):
        step = norm / form(direction, direction, 1)
        for i, c in enumerate(direction):
            pressure[i] = pressure[i] + step * c
        if sweep < 2:
            moved = [zero] + direction
            old = scaled + [zero] * (len(moved) - len(scaled))
            scaled = [a - step * b for a, b in zip(old, moved)]
            following = form(scaled, scaled, 0)
            ratio = following / norm
            direction = [a + ratio * b for a, b in zip(scaled, direction + [zero])]
            norm = following
    return pressure


def gradient_kernel(all_moments, core, beside, pressure, table, p):
    summed = jnp.sum(all_moments[...], axis=0)
    coef = coefficients([jnp.broadcast_to(summed[:, k:k + 1], (8, 128)) for k in range(6)])
    coef = [jnp.broadcast_to(c[:1], (64, 128)) for c in coef]
    lane = plane_lanes()
    first, last = lane == 0, lane == 127

    def combine(ref, r):
        return coef[0] * ref[0, r] + coef[1] * ref[1, r] + coef[2] * ref[2, r]
    for r in range(3, 13):
        p[r, 0:8] = jnp.zeros((8, 128), f32)
        p[r, 72:80] = jnp.zeros((8, 128), f32)
        p[r, MID] = combine(core, r - 3)
    for x in range(8):
        r = x + 4
        pair = (p[r, MID], combine(beside, x))
        pressure[pl.ds(x, 64, stride=8), :] = pair[0]
        put_table(table, 0, x, 0.5 * (p[r + 1, MID] - p[r - 1, MID]))
        put_table(table, 1, x, 0.5 * (up_pair(pair, last)[0] - down_pair(pair, first)[0]))
        put_table(table, 2, x, 0.5 * (p[r, UP] - p[r, DOWN]))


def gradients(all_moments, core, beside):
    return pl.pallas_call(
        gradient_kernel,
        out_shape=(S((512, 128), f32), S((NW, 48, 256), bf16)),
        in_specs=[VSPEC] * 3,
        out_specs=(VSPEC,) * 2,
        scratch_shapes=[pltpu.VMEM((16, 80, 128), f32)],
        compiler_params=VM,
        name="gradients",
    )(all_moments, core, beside)


def arrange_kernel(*refs):
    for i, out in enumerate(refs[3:]):
        for d in range(3):
            out[d * PR:(d + 1) * PR, :] = refs[d][i * PR:(i + 1) * PR, :]


def arrange(*arrays):
    return pl.pallas_call(
        arrange_kernel,
        out_shape=(S((3 * PR, 128), f32),) * 5,
        in_specs=[VSPEC] * 3,
        out_specs=(VSPEC,) * 5,
        compiler_params=VM,
        name="arrange",
    )(*arrays)


def place_kernel(back_refs, groups, *refs):
    n = back_refs
    backs, (pos_a, pos_b), out = refs[:n], refs[n:n + 2], refs[n + 2]
    stage, found, tiles, zeros, sem_zero, sem_tile = refs[n + 3:]
    hx, hy = lax.axis_index("gx"), lax.axis_index("gy")
    zeros[...] = jnp.zeros_like(zeros)

    def tile_at(t):
        return out.at[:, 0, pl.ds(pl.multiple_of(t * 8, 8), 8), :]

    def far(t):
        return jnp.abs(t - hx) > 2
    for t in range(16):
        @pl.when(far(t))
        def _():
            pltpu.make_async_copy(zeros, tile_at(t), sem_zero.at[t]).start()
    where = {-2: 0, -1: 1, 0: 2, 1: 3, 2: 4}
    for g, runs in enumerate(groups):
        side = lax.rem(hx // abs(runs[0][0]), 2) == 0
        pair = (backs[0], backs[1]) if g == 0 else (backs[3], backs[4])
        up = lax.rem(hy, 2) == 0
        sources = (jnp.where(up, 2 * PR, 0), PR, jnp.where(up, 0, 2 * PR))
        for ref, first in zip(pair, (jnp.where(side, 3 * PR, 0), jnp.where(side, 0, 3 * PR))):
            for d in range(3):
                to = pl.multiple_of(first + d * PR, 8)
                stage[pl.ds(to, PR), :] = ref[pl.ds(pl.multiple_of(sources[d], 8), PR), :]
        _, dy0, first, count = runs[2]
        for d in range(count):
            src = pl.multiple_of(sources[dy0 + 1 + d], 8)
            stage[(first + d) * PR:(first + d + 1) * PR, :] = backs[2][pl.ds(src, PR), :]
        if g == 1:
            stage[7 * PR:8 * PR, :] = jnp.zeros((PR, 128), f32)
        pos_ref = (pos_a, pos_b)[g]

        def chunk(c):
            k = pos_ref[c]
            at, src = k & 127, k >> 7
            acc = [jnp.zeros((8, 128), f32) for _ in range(3)]
            for v in range(CH):
                here = src == v
                for f in range(3):
                    got = jnp.take_along_axis(stage[pl.ds(f * CH + v, 8, stride=PR), :], at, axis=1)
                    acc[f] = jnp.where(here, got, acc[f])
            for f in range(3):
                found[g, f, c] = acc[f]
        unrolled(CH, 8, chunk)
    row = lax.broadcasted_iota(i32, (8, 128), 0)
    for dx in (-2, -1, 0, 1, 2):
        pieces = [(g, run) for g, runs in enumerate(groups) for run in runs if run[0] == dx]
        turned = []
        for g, (_, dy0, first, count) in pieces:
            shift = lax.rem(hy + dy0 - first + 16, 8)
            low = hy + dy0
            turned.append((g, shift, (row >= low) & (row < low + count)))
        for f in range(3):
            for c in range(CH):
                got = jnp.zeros((8, 128), f32)
                for g, shift, mask in turned:
                    got = jnp.where(mask, pltpu.roll(found[g, f, c], shift, 0), got)
                tiles[where[dx], f, :, c * 128:(c + 1) * 128] = got

        @pl.when((hx + dx >= 0) & (hx + dx < NGX))
        def _():
            pltpu.make_async_copy(tiles.at[where[dx]], tile_at(hx + dx), sem_tile.at[where[dx]]).start()
    for t in range(16):
        @pl.when(far(t))
        def _():
            pltpu.make_async_copy(zeros, tile_at(t), sem_zero.at[t]).wait()
    for dx in (-2, -1, 0, 1, 2):
        @pl.when((hx + dx >= 0) & (hx + dx < NGX))
        def _():
            pltpu.make_async_copy(tiles.at[where[dx]], tile_at(hx + dx), sem_tile.at[where[dx]]).wait()


def place_forces(backs, pos):
    return pl.pallas_call(
        functools.partial(place_kernel, len(backs), GROUPS),
        out_shape=S((3, 1, 128, 3072), f32),
        in_specs=[VSPEC] * (len(backs) + 2),
        out_specs=pl.BlockSpec(memory_space=pl.ANY),
        scratch_shapes=[
            pltpu.VMEM((8 * PR, 128), f32),
            pltpu.VMEM((2, 3, CH, 8, 128), f32),
            pltpu.VMEM((5, 3, 8, 3072), f32),
            pltpu.VMEM((3, 8, 3072), f32),
            pltpu.SemaphoreType.DMA((16,)),
            pltpu.SemaphoreType.DMA((5,)),
        ],
        compiler_params=VM,
        name="place_forces",
    )(*backs, *pos)


def exchange(x, axis, by, which):
    count = {"gx": NGX, "gy": NGY}[axis]
    pairs = [(i, i + by) for i in range(count - by) if (i // by) % 2 == which]
    return lax.ppermute(x, axis, pairs + [(j, i) for i, j in pairs])


def per_device(particle_data, particle_cells, slot_counts, fluid_velocity):
    two_0, two_1, zero_a, keys_a = sort_blocks(GROUPS[0], particle_data, particle_cells, slot_counts)
    two_0, two_1 = exchange(two_0, "gx", 2, 0), exchange(two_1, "gx", 2, 1)
    one_0, one_1, zero_b, keys_b = sort_blocks(GROUPS[1], particle_data, particle_cells, slot_counts)
    one_0, one_1 = exchange(one_0, "gx", 1, 0), exchange(one_1, "gx", 1, 1)
    along = [two_0, two_1, jnp.concatenate([zero_a, zero_b], axis=0), one_0, one_1]
    below, mine, above = [jnp.concatenate([a[d * BR:(d + 1) * BR] for a in along], axis=0) for d in range(3)]
    up = lax.rem(lax.axis_index("gy"), 2) == 0
    sides = [
        exchange(jnp.where(up, above, below), "gy", 1, 0),
        exchange(jnp.where(up, below, above), "gy", 1, 1),
    ]
    bases = tuple(range(0, 5 * BR, BR))
    acc = deposit([mine], bases, 8)
    table, own, send_0, send_1, token = deposit(sides, bases, 4, acc, fluid_velocity.reshape(3, 512, 128))
    rows = (own, send_0, send_1, exchange(send_0, "gx", 1, 0), exchange(send_1, "gx", 1, 1))
    *pos, token = inverse(keys_a, keys_b, token)
    packed = pack_edges(rows, token)
    core, beside, moments = sweeps(rows, packed, exchange(packed, "gy", 1, 0), exchange(packed, "gy", 1, 1))
    everyone = lax.all_to_all(moments, ("gx", "gy"), 0, 0)
    pressure, slopes = gradients(everyone, core, beside)
    far_0, far_1, token = interp(sides, bases, table, slopes, 4, token, 2)
    back = [exchange(far_0, "gy", 1, 0), exchange(far_1, "gy", 1, 1)]
    near, _ = interp([mine], bases, table, slopes, 8, token, 1)
    blocks = list(arrange(back[0], near, back[1]))
    for i, (by, which) in ((0, (2, 0)), (1, (2, 1)), (3, (1, 0)), (4, (1, 1))):
        blocks[i] = exchange(blocks[i], "gx", by, which)
    drag = place_forces(blocks, pos)
    return pressure.reshape(64, 8, 128), drag


def solution(mesh):
    return jax.shard_map(
        per_device,
        mesh=mesh,
        in_specs=(
            P(None, ("gx", "gy"), None, None),
            P(None, ("gx", "gy"), None, None),
            P(("gx", "gy"), None),
            P(None, None, "gx", "gy"),
        ),
        out_specs=(P(None, "gx", "gy"), P(None, ("gx", "gy"), None, None)),
        check_vma=False,
    )
```

```python
import functools
import jax
import jax.numpy as jnp
from jax import lax
from jax.experimental import pallas as pl
from jax.experimental.pallas import tpu as pltpu
from jax.sharding import PartitionSpec as P

f32, bf16, i32 = jnp.float32, jnp.bfloat16, jnp.int32
CH = 24
BR = 152
WL = 16
NW = 32
SPAN = WL * 128
PR = 3 * CH
VM = pltpu.CompilerParams(vmem_limit_bytes=24 * 1024 * 1024)
VSPEC = pl.BlockSpec(memory_space=pltpu.VMEM)
S = jax.ShapeDtypeStruct
TOKEN = S((8, 128), f32)


def sort_network(x):
    lane = lax.broadcasted_iota(i32, (1, 8, 128), 2)
    flipped = None
    for merge in range(1, 13):
        if merge < 12:
            if merge >= 5:
                want = (lane >> (merge - 5)) & 1
                mask = -want
            else:
                mask = jnp.asarray(-((lax.broadcasted_iota(i32, (32, 8, 128), 0) >> merge) & 1))
        else:
            mask = None
        if mask is not None:
            x = x ^ mask
        for bit in range(merge - 1, -1, -1):
            if bit < 5:
                step = 1 << bit
                y = x.reshape(32 // (2 * step), 2, step, 8, 128)
                a, b = y[:, 0], y[:, 1]
                x = jnp.stack([jnp.minimum(a, b), jnp.maximum(a, b)], axis=1).reshape(32, 8, 128)
            else:
                step = 1 << (bit - 5)
                up = (lane & step) != 0
                other = jnp.take_along_axis(x, jnp.broadcast_to(lane ^ step, x.shape), axis=2)
                x = jnp.where(up, jnp.maximum(x, other), jnp.minimum(x, other))
        if mask is not None:
            x = x ^ mask
    return x


def lanes_to_chunks(x):
    lane = lax.broadcasted_iota(i32, (1, 8, 128), 2)
    for bit in range(5):
        step = 1 << bit
        y = x.reshape(32 // (2 * step), 2, step, 8, 128)
        a, b = y[:, 0], y[:, 1]
        up = ((lane & step) != 0)[:, None]
        na = jnp.where(up, pltpu.roll(b, step, 3), a)
        nb = jnp.where(up, b, pltpu.roll(a, 128 - step, 3))
        x = jnp.stack([na, nb], axis=1).reshape(32, 8, 128)
    for bit in range(2):
        step, far = 1 << bit, 32 << bit
        y = x.reshape(32 // (2 * step), 2, step, 8, 128)
        a, b = y[:, 0], y[:, 1]
        up = ((lane & far) != 0)[:, None]
        na = jnp.where(up, pltpu.roll(b, far, 3), a)
        nb = jnp.where(up, b, pltpu.roll(a, 128 - far, 3))
        x = jnp.stack([na, nb], axis=1).reshape(32, 8, 128)
    return jnp.stack([x[(c % 8) * 4 + c // 8] for c in range(32)], axis=0)


GROUPS = (((-2, -1, 0, 3), (2, -1, 3, 3), (0, -1, 6, 2)), ((-1, -1, 0, 3), (1, -1, 3, 3), (0, 1, 6, 1)))
NGX, NGY = 16, 8


def unrolled(count, by, body):
    def several(i, _):
        for j in range(by):
            body(i * by + j)
        return 0
    lax.fori_loop(0, count // by, several, 0)


def row_mask(first, count):
    row = lax.broadcasted_iota(i32, (8, 128), 0)
    return (row >= first) & (row < first + count)


def sort_kernel(runs, n_out, data_ref, cells_ref, counts_ref, *rest):
    outs, pos_ref = rest[:n_out], rest[n_out]
    data_v, cells_v, key_s, pay_s, out_s, sems = rest[n_out + 1:]
    hx, hy = lax.axis_index("gx"), lax.axis_index("gy")
    copies = []
    for t, (dx, _, _, _) in enumerate(runs):
        tile = pl.ds(pl.multiple_of(jnp.clip(hx + dx, 0, NGX - 1) * 8, 8), 8)
        copies.append(pltpu.make_async_copy(cells_ref.at[:, 0, tile, :], cells_v.at[t], sems.at[2 * t]))
    for t, (dx, _, _, _) in enumerate(runs):
        tile = pl.ds(pl.multiple_of(jnp.clip(hx + dx, 0, NGX - 1) * 8, 8), 8)
        copies.append(pltpu.make_async_copy(data_ref.at[:, 0, tile, :], data_v.at[t], sems.at[2 * t + 1]))
    for copy in copies:
        copy.start()
    lane = lax.broadcasted_iota(i32, (8, 128), 1)
    row = lax.broadcasted_iota(i32, (8, 128), 0)
    counts = jnp.zeros((8, 128), i32)
    for dx, dy0, first, count in runs:
        for i in range(count):
            bx, by = hx + dx, hy + dy0 + i
            valid = (bx >= 0) & (bx < NGX) & (by >= 0) & (by < NGY)
            n = counts_ref[0, jnp.clip(bx * NGY + by, 0, NGX * NGY - 1)]
            counts = jnp.where(row == first + i, jnp.where(valid, n, 0), counts)
    shifts = [lax.rem(first - (hy + dy0) + 16, 8) for _, dy0, first, _ in runs]
    masks = [row_mask(first, count) for _, _, first, count in runs]
    for copy in copies[:len(runs)]:
        copy.wait()

    def gathered(ref, f, c):
        got = None
        for t in range(len(runs)):
            x = pltpu.roll(ref[t, f, :, c * 128:(c + 1) * 128], shifts[t], 0)
            got = x if got is None else jnp.where(masks[t], x, got)
        return got

    rows = []
    for c in range(32):
        slot = lane + c * 128
        if c < CH:
            h, col = gathered(cells_v, 0, c), gathered(cells_v, 1, c)
            live = slot < counts
            cell = (((col >> 7) * 64 + h) << 7) + (col & 127)
            cell = jnp.where(live, cell, 65536)
            rows.append((cell << 12) + slot)
        else:
            rows.append((1 << 29) + slot)
    keys = lanes_to_chunks(sort_network(jnp.stack(rows, axis=0)))
    key_s[...] = keys[:CH]
    pos_ref[...] = keys[:CH]
    for copy in copies[len(runs):]:
        copy.wait()
    for c in range(CH):
        for f in range(5):
            pay_s[f, c] = jnp.where(lane + c * 128 < counts, gathered(data_v, f, c), 0.0)

    def chunk(c):
        k = key_s[c]
        slot = k & 4095
        at, src = slot & 127, slot >> 7
        acc = [jnp.zeros((8, 128), f32) for _ in range(5)]
        for v in range(CH):
            here = src == v
            for f in range(5):
                got = jnp.take_along_axis(pay_s[f, v], at, axis=1)
                acc[f] = jnp.where(here, got, acc[f])
        for f in range(5):
            out_s[pl.ds(f * CH + c, 8, stride=BR), :] = acc[f]
        out_s[pl.ds(5 * CH + c, 8, stride=BR), :] = (k >> 12).astype(f32)
    unrolled(CH, 4, chunk)
    low = lane < 64
    bound = jnp.where(low, lane, lane - 63) * SPAN
    total = jnp.zeros((8, 128), i32)
    for c in range(CH):
        cell = key_s[c] >> 12
        last = jnp.broadcast_to(cell[:, 127:128], (8, 128))
        start = jnp.broadcast_to(cell[:, 0:1], (8, 128))
        total = total + jnp.where(jnp.where(low, last, start) < bound, 1, 0)
    for r in range(8):
        out_s[pl.ds(6 * CH + r, 8, stride=BR), :] = total.astype(f32)
    side = lax.rem(hx // abs(runs[0][0]), 2) == 0
    for out, first in ((outs[0], jnp.where(side, 3 * BR, 0)), (outs[1], jnp.where(side, 0, 3 * BR))):
        out[...] = out_s[pl.ds(pl.multiple_of(first, 8), 3 * BR), :]
    _, _, first, count = runs[2]
    outs[2][...] = out_s[first * BR:(first + count) * BR, :]


def inverse_kernel(keys_a, keys_b, after, pos_a, pos_b, token):
    token[...] = after[...]
    place = lax.broadcasted_iota(i32, (CH, 8, 128), 0) * 128 + lax.broadcasted_iota(i32, (CH, 8, 128), 2)
    rest = jnp.full((32 - CH, 8, 128), 1 << 29, i32)
    for keys, pos in ((keys_a, pos_a), (keys_b, pos_b)):
        back = jnp.concatenate([((keys[...] & 4095) << 12) + place, rest], axis=0)
        pos[...] = lanes_to_chunks(sort_network(back))[:CH] & 4095


def inverse(keys_a, keys_b, after):
    shape = jax.ShapeDtypeStruct((CH, 8, 128), i32)
    return pl.pallas_call(
        inverse_kernel,
        out_shape=(shape, shape, TOKEN),
        in_specs=[VSPEC] * 3,
        out_specs=(VSPEC,) * 3,
        compiler_params=VM,
        cost_estimate=pl.CostEstimate(flops=10**9, bytes_accessed=2 * 10**7, transcendentals=0),
        name="inverse",
    )(keys_a, keys_b, after)


def sort_blocks(runs, data, cells, counts):
    shapes = [jax.ShapeDtypeStruct((count * BR, 128), f32) for _, _, _, count in runs]
    shapes.append(jax.ShapeDtypeStruct((CH, 8, 128), i32))
    n = len(runs)
    return pl.pallas_call(
        functools.partial(sort_kernel, runs, n),
        out_shape=tuple(shapes),
        in_specs=[pl.BlockSpec(memory_space=pltpu.HBM)] * 2 + [pl.BlockSpec(memory_space=pltpu.SMEM)],
        out_specs=(pl.BlockSpec(memory_space=pltpu.VMEM),) * (n + 1),
        scratch_shapes=[
            pltpu.VMEM((n, 5, 8, 3072), f32),
            pltpu.VMEM((n, 2, 8, 3072), i32),
            pltpu.VMEM((CH, 8, 128), i32),
            pltpu.VMEM((5, CH, 8, 128), f32),
            pltpu.VMEM((8 * BR, 128), f32),
            pltpu.SemaphoreType.DMA((2 * n,)),
        ],
        compiler_params=pltpu.CompilerParams(vmem_limit_bytes=56 * 1024 * 1024),
        name="sort_blocks",
    )(data, cells, counts)


def load_offsets(refs, off_v, off_s, sem):
    for j, (ref, base) in enumerate(refs):
        off_v[j:j + 1, :] = ref[base + 6 * CH:base + 6 * CH + 1, :].astype(i32)
    copy = pltpu.make_async_copy(off_v, off_s, sem)
    copy.start()
    copy.wait()


def wide(row, rows):
    return jnp.broadcast_to(row, (rows, 128))


def split_cell(cell):
    line = jnp.floor(cell * (1.0 / 128.0))
    return line, cell - line * 128.0


def width_onehot(wid, iota):
    w16 = wide(wid, 16).astype(bf16)
    w = jnp.concatenate([w16] * 8, axis=0)
    return jnp.where(w == iota, jnp.asarray(1.0, bf16), jnp.asarray(0.0, bf16))


def deposit_kernel(nref, bases, unroll, use_acc, *refs):
    blocks = [(refs[i], b) for i in range(nref) for b in bases]
    nb = len(blocks)
    rest = refs[nref:]
    if use_acc:
        prev, fluid, table, own, send_0, send_1, token, out, flux, pre, off_v, off_s, sem = rest
    else:
        out, pre, off_v, off_s, sem = rest
    load_offsets(blocks, off_v, off_s, sem)
    for j, (ref, base) in enumerate(blocks):
        vol = ref[base:base + CH, :]
        coef = ref[base + CH:base + 2 * CH, :]
        vals = [vol, coef] + [coef * ref[base + (2 + d) * CH:base + (3 + d) * CH, :] for d in range(3)]
        for k, v in enumerate(vals):
            hi = v.astype(bf16).astype(f32)
            pre[j, k] = hi
            pre[j, 5 + k] = v - hi
        line, wid = split_cell(ref[base + 5 * CH:base + 6 * CH, :])
        pre[j, 10] = line
        pre[j, 11] = wid
    iota = lax.broadcasted_iota(i32, (128, 128), 0).astype(f32).astype(bf16)
    iota16 = lax.broadcasted_iota(i32, (16, 128), 0).astype(f32).astype(bf16)
    zero = jnp.zeros((16, 128), bf16)

    def operands(j, c, w):
        rel = jnp.clip(pre[j, 10, pl.ds(c, 1), :] - (w * WL).astype(f32), -1.0, 16.0)
        mask = wide(rel, 16).astype(bf16) == iota16
        a = jnp.concatenate(
            [jnp.where(mask, wide(pre[j, k, pl.ds(c, 1), :], 16).astype(bf16), zero) for k in range(10)], axis=0)
        return a, width_onehot(pre[j, 11, pl.ds(c, 1), :], iota)

    def product(a, b):
        p = lax.dot_general(a, b, (((1,), (1,)), ((), ())), preferred_element_type=f32)
        return p

    def halves(p):
        return (p[:80] + p[80:]).reshape(5, WL, 128)

    def windows(i, more):
        for u in range(unroll):
            w = i * unroll + u
            total = None
            for j in range(nb):
                first = jnp.minimum(off_s[j, w], CH - 2)
                more = jnp.maximum(more, off_s[j, 64 + w] - first)
                a0, b0 = operands(j, first, w)
                a1, b1 = operands(j, first + 1, w)
                p = product(jnp.concatenate([a0, a1], axis=1), jnp.concatenate([b0, b1], axis=1))
                total = p if total is None else total + p
            total = halves(total)
            rows = pl.ds(pl.multiple_of(w * WL, WL), WL)
            if use_acc:
                total = total + prev[:, rows, :]
            out[:, rows, :] = total
        return more
    more = lax.fori_loop(0, NW // unroll, windows, jnp.int32(0))

    @pl.when(more > 2)
    def _():
        def window(w, _):
            rows = pl.ds(pl.multiple_of(w * WL, WL), WL)

            def block(j, _):
                def step(c, _):
                    a, b = operands(j, c, w)
                    out[:, rows, :] += halves(product(a, b))
                    return 0
                return lax.fori_loop(jnp.minimum(off_s[j, w], CH - 2) + 2, off_s[j, 64 + w], step, 0)
            return lax.fori_loop(0, nb, block, 0)
        lax.fori_loop(0, NW, window, 0)


    if use_acc:
        fields(out, fluid, table, own, send_0, send_1, flux)
        token[...] = jnp.zeros_like(token)


def deposit(arrays, bases, unroll, prev=None, fluid=None):
    nb = len(arrays) * len(bases)
    args = list(arrays) + ([] if prev is None else [prev, fluid])
    total = S((5, 512, 128), f32)
    sent = S((SENT, 64, 128), f32)
    shapes = (S((NW, 48, 256), bf16), S((2, 8, 64, 128), f32), sent, sent, TOKEN)
    scratch = [
        pltpu.VMEM((nb, 12, CH, 128), f32),
        pltpu.VMEM((nb, 128), i32),
        pltpu.SMEM((nb, 128), i32),
        pltpu.SemaphoreType.DMA,
    ]
    if prev is not None:
        scratch = [pltpu.VMEM((5, 512, 128), f32), pltpu.VMEM((8, 64, 128), f32)] + scratch
    return pl.pallas_call(
        functools.partial(deposit_kernel, len(arrays), bases, unroll, prev is not None),
        out_shape=total if prev is None else shapes,
        in_specs=[VSPEC] * len(args),
        out_specs=VSPEC if prev is None else (VSPEC,) * 5,
        scratch_shapes=scratch,
        compiler_params=VM,
        cost_estimate=pl.CostEstimate(flops=10**9 * nb, bytes_accessed=3 * 10**6 * nb, transcendentals=0),
        name="deposit",
    )(*args)


def interp_kernel(nref, bases, unroll, *refs):
    blocks = [(refs[i], b) for i in range(nref) for b in bases]
    nb = len(blocks)
    fast, slope, _ = refs[nref:nref + 3]
    outs = refs[nref + 3:-6]
    token, pre, acc, off_v, off_s, sem = refs[-6:]
    each = nb // len(outs)
    token[...] = jnp.zeros_like(token)
    load_offsets(blocks, off_v, off_s, sem)
    for j, (ref, base) in enumerate(blocks):
        line, wid = split_cell(ref[base + 5 * CH:base + 6 * CH, :])
        pre[j, 0] = line
        pre[j, 1] = wid
        pre[j, 2] = ref[base + CH:base + 2 * CH, :]
        pre[j, 3] = -ref[base:base + CH, :]
    acc[...] = jnp.zeros_like(acc)
    iota = lax.broadcasted_iota(i32, (128, 128), 0).astype(f32).astype(bf16)
    iota16 = lax.broadcasted_iota(i32, (16, 128), 0).astype(f32)

    def visit(j, c, w, width, tab):
        scales, hots = [], []
        for i in range(width):
            at = pl.ds(c + i, 1)
            mask = wide(pre[j, 0, at, :] - (w * WL).astype(f32), 16) == iota16
            scales.append([jnp.where(mask, wide(pre[j, 2 + s, at, :], 16), 0.0) for s in range(2)])
            b = width_onehot(pre[j, 1, at, :], iota)
            hots.append(jnp.concatenate([b, b], axis=0))
        hot = hots[0] if width == 1 else jnp.concatenate(hots, axis=1)
        g = jnp.dot(tab, hot, preferred_element_type=f32)
        for i in range(width):
            for k in range(3):
                lanes = slice(i * 128, (i + 1) * 128)
                part = scales[i][0] * g[k * 16:k * 16 + 16, lanes]
                part = part + scales[i][1] * g[48 + k * 16:64 + k * 16, lanes]
                acc[j, c + i, k] += part[:8] + part[8:]

    def windows(i, more):
        for u in range(unroll):
            w = i * unroll + u
            tab = jnp.concatenate([fast[w], slope[w]], axis=0)
            for j in range(nb):
                first = jnp.minimum(off_s[j, w], CH - 2)
                more = jnp.maximum(more, off_s[j, 64 + w] - first)
                visit(j, first, w, 2, tab)
        return more
    more = lax.fori_loop(0, NW // unroll, windows, jnp.int32(0))

    @pl.when(more > 2)
    def _():
        def window(w, _):
            tab = jnp.concatenate([fast[w], slope[w]], axis=0)

            def block(j, _):
                def step(c, _):
                    visit(j, c, w, 1, tab)
                    return 0
                return lax.fori_loop(jnp.minimum(off_s[j, w], CH - 2) + 2, off_s[j, 64 + w], step, 0)
            return lax.fori_loop(0, nb, block, 0)
        lax.fori_loop(0, NW, window, 0)
    for j, (ref, base) in enumerate(blocks):
        coef = ref[base + CH:base + 2 * CH, :]
        for k in range(3):
            vel = ref[base + (2 + k) * CH:base + (3 + k) * CH, :]
            at = (j % each) * PR + k * CH
            outs[j // each][at:at + CH, :] = jnp.sum(acc[j, :, k], axis=1) - coef * vel


def interp(arrays, bases, fast, slope, unroll, after, n_out):
    nb = len(arrays) * len(bases)
    args = list(arrays) + [fast, slope, after]
    return pl.pallas_call(
        functools.partial(interp_kernel, len(arrays), bases, unroll),
        out_shape=(S((nb // n_out * PR, 128), f32),) * n_out + (TOKEN,),
        in_specs=[VSPEC] * len(args),
        out_specs=(VSPEC,) * (n_out + 1),
        scratch_shapes=[
            pltpu.VMEM((nb, 4, CH, 128), f32),
            pltpu.VMEM((nb, CH, 3, 8, 128), f32),
            pltpu.VMEM((nb, 128), i32),
            pltpu.SMEM((nb, 128), i32),
            pltpu.SemaphoreType.DMA,
        ],
        compiler_params=VM,
        cost_estimate=pl.CostEstimate(flops=10**9 * nb, bytes_accessed=3 * 10**6 * nb, transcendentals=0),
        name="interp",
    )(*args)

TIME_STEP = 0.1
SHIFT = 0.05


def put_table(table, k, x, values):
    hi = values.astype(bf16)
    lo = (values - hi.astype(f32)).astype(bf16)
    for q in range(4):
        table[4 * x + q, k * 16:k * 16 + 16, 0:128] = hi[16 * q:16 * q + 16]
        table[4 * x + q, k * 16:k * 16 + 16, 128:256] = lo[16 * q:16 * q + 16]


def up_z(x):
    return jnp.concatenate([x[1:], jnp.zeros_like(x[:1])], axis=0)


def down_z(x):
    return jnp.concatenate([jnp.zeros_like(x[:1]), x[:-1]], axis=0)


def plane_lanes():
    return lax.broadcasted_iota(i32, (64, 128), 1)


def is_even(axis):
    return lax.rem(lax.axis_index(axis), 2) == 0


def turn(x, by):
    return x if by % 128 == 0 else pltpu.roll(x, by % 128, 1)


SENT = 9


def fields(acc, fluid, table, own, send_0, send_1, flux):
    even = is_even("gx")
    lane = plane_lanes()
    ends = jnp.zeros((64, 128), f32)
    for x in range(8):
        at = slice(x * 64, x * 64 + 64)
        fraction = acc[0, at, :]
        drag = acc[1, at, :]
        porosity = 1.0 / (1.0 + fraction)
        fluxes = []
        for d in range(3):
            fluid_d = fluid[d, pl.ds(x, 64, stride=8), :]
            predicted = fluid_d + TIME_STEP * (1.0 + fraction) * (acc[2 + d, at, :] - drag * fluid_d)
            put_table(table, d, x, predicted)
            fluxes.append(porosity * predicted)
        flux[x] = fluxes[0]
        fy, fz = fluxes[1:]
        along_y = jnp.where(lane < 127, turn(fy, -1), 0.0) - jnp.where(lane > 0, turn(fy, 1), 0.0)
        own[0, x] = porosity
        own[1, x] = -0.5 * (along_y + (up_z(fz) - down_z(fz)))
        mid = 8 * (x + 4)
        ends = jnp.where((lane == mid) | (lane == mid - 1), turn(fy, mid), ends)
    for x in range(8):
        along_x = (flux[x + 1] if x < 7 else 0.0) - (flux[x - 1] if x > 0 else 0.0)
        own[1, x] = own[1, x] - 0.5 * along_x
    low = [own[0, x] for x in range(4)] + [own[1, x] for x in range(3)] + [flux[0], ends]
    high = [own[0, x] for x in range(4, 8)] + [own[1, x] for x in range(5, 8)] + [flux[7], ends]
    for i in range(SENT):
        send_0[i] = jnp.where(even, high[i], low[i])
        send_1[i] = jnp.where(even, low[i], high[i])


def extended(refs):
    own, sent_0, sent_1, got_0, got_1 = refs
    even = is_even("gx")

    def below(i):
        return jnp.where(even, got_1[i], got_0[i])

    def above(i):
        return jnp.where(even, got_0[i], got_1[i])

    def porosity(r):
        return below(r) if r < 4 else own[0, r - 4] if r < 12 else above(r - 12)

    def source(r):
        if r == 3:
            return below(6) - 0.5 * jnp.where(even, sent_1[7], sent_0[7])
        if r == 4:
            return own[1, 0] + 0.5 * below(7)
        if r == 11:
            return own[1, 7] - 0.5 * above(7)
        if r == 12:
            return above(4) + 0.5 * jnp.where(even, sent_0[7], sent_1[7])
        return below(3 + r) if r < 4 else own[1, r - 4] if r < 12 else above(r - 8)

    def ends():
        lane = plane_lanes()
        beside = jnp.where((lane >= 92) & (lane < 124), turn(above(8), 64), turn(below(8), 64))
        return jnp.where((lane >= 28) & (lane < 92), sent_0[8], beside)
    return porosity, source, ends


def pack_kernel(own, sent_0, sent_1, got_0, got_1, after, out):
    del after
    porosity, source, ends = extended((own, sent_0, sent_1, got_0, got_1))
    lane = plane_lanes()
    for f, (rows, get) in enumerate(((range(16), porosity), (range(1, 15), source))):
        got = jnp.zeros((64, 128), f32)
        for r in rows:
            place = (lax.rem(lane + 132 - 8 * r, 128)) < 8
            got = jnp.where(place, turn(get(r), 8 * r), got)
        out[f] = got
    out[2] = ends()


def pack_edges(refs, after):
    return pl.pallas_call(
        pack_kernel,
        out_shape=S((3, 64, 128), f32),
        in_specs=[VSPEC] * 6,
        out_specs=VSPEC,
        compiler_params=VM,
        name="pack_edges",
    )(*refs, after)


def face(e, n):
    return 2.0 * e * n / jnp.maximum(e + n, 1e-30)


def up_pair(pair, last):
    a, b = (pltpu.roll(x, 127, 1) for x in pair)
    return jnp.where(last, b, a), jnp.where(last, a, b)


def down_pair(pair, first):
    a, b = (pltpu.roll(x, 1, 1) for x in pair)
    return jnp.where(first, b, a), jnp.where(first, a, b)


MID, UP, DOWN = pl.ds(8, 64), pl.ds(9, 64), pl.ds(7, 64)


def sweeps_kernel(own, sent_0, sent_1, got_0, got_1, packed, edge_0, edge_1, core, beside, moments, vs, por, src, wx, wy, wz,
                  diag, inv):
    porosity, source, _ = extended((own, sent_0, sent_1, got_0, got_1))
    lane = plane_lanes()
    first, last = lane == 0, lane == 127
    keep = (lane < 4) | (lane >= 124)
    even_y = is_even("gy")

    def above(f):
        return jnp.where(even_y, edge_0[f], edge_1[f])

    def below(f):
        return jnp.where(even_y, edge_1[f], edge_0[f])
    part = lane & 7

    def crossed(from_below, from_above):
        return jnp.where(part == 0, 0.5 * turn(from_below, 1), jnp.where(part == 7, -0.5 * turn(from_above, -1), 0.0))
    side_e = jnp.where(part < 4, above(0), below(0))
    side_b = jnp.where(part < 4, above(1), below(1)) + crossed(packed[2], packed[2])
    core_b = crossed(below(2), above(2))
    for ref in (por, wz):
        for h in range(2):
            for r in range(16):
                ref[h, r, 0:8] = jnp.zeros((8, 128), f32)
                ref[h, r, 72:80] = jnp.zeros((8, 128), f32)
    for k in range(3):
        for r in range(1, 15):
            for h in range(2):
                vs[k, h, r, 0:8] = jnp.zeros((8, 128), f32)
                vs[k, h, r, 72:80] = jnp.zeros((8, 128), f32)
    for r in range(16):
        por[0, r, MID] = porosity(r)
        por[1, r, MID] = jnp.where(keep, turn(side_e, -8 * r), 0.0)
        if 0 < r < 15:
            src[0, r] = source(r) + jnp.where(first | last, turn(core_b, -8 * r), 0.0)
            src[1, r] = jnp.where(keep, turn(side_b, -8 * r), 0.0)

    def faces(r):
        pair = [por[h, r, MID] for h in range(2)]
        up = up_pair(pair, last)
        for h in range(2):
            wx[h, r] = face(pair[h], por[h, r + 1, MID])
            wy[h, r] = face(pair[h], up[h])
            wz[h, r, MID] = face(pair[h], por[h, r, UP])
    for r in range(15):
        faces(r)

    def keep_plane(k, h, r, v):
        vs[k, h, r, MID] = v
        if h == 0 and 3 <= r < 13:
            core[k, r - 3] = v
        if h == 1 and 4 <= r < 12:
            beside[k, r - 4] = v

    def sources(r):
        y = [wy[h, r] for h in range(2)]
        y_down = down_pair(y, first)
        for h in range(2):
            e = por[h, r, MID]
            d = SHIFT * e + wx[h, r] + wx[h, r - 1] + y[h] + y_down[h] + wz[h, r, MID] + wz[h, r, DOWN]
            outside = e == 0.0
            i = jnp.where(outside, 0.0, 1.0 / jnp.where(outside, 1.0, d))
            diag[h, r] = d
            inv[h, r] = i
            keep_plane(0, h, r, src[h, r] * i)
    for r in range(1, 15):
        sources(r)

    def spread(k, r, halves):
        pair = [vs[k, h, r, MID] for h in range(2)]
        y = [wy[h, r] for h in range(2)]
        up = up_pair(pair, last)
        down = down_pair([a * b for a, b in zip(y, pair)], first)
        made = []
        for h in range(halves):
            total = wx[h, r] * vs[k, h, r + 1, MID] + wx[h, r - 1] * vs[k, h, r - 1, MID]
            total = total + y[h] * up[h] + down[h]
            total = total + wz[h, r, MID] * vs[k, h, r, UP] + wz[h, r, DOWN] * vs[k, h, r, DOWN]
            made.append((diag[h, r] * pair[h] - total) * inv[h, r])
        return made

    for k, (lo, hi) in ((0, (2, 14)), (1, (3, 13))):
        for r in range(lo, hi):
            for h, v in enumerate(spread(k, r, 2)):
                keep_plane(k + 1, h, r, v)

    def sums(r, total):
        d = diag[0, r]
        v0, v1, v2 = (vs[k, 0, r, MID] for k in range(3))
        v3, = spread(2, r, 1)
        d0, d1, d2 = d * v0, d * v1, d * v2
        terms = (d0 * v0, d0 * v1, d1 * v1, d1 * v2, d2 * v2, d2 * v3)
        return tuple(t + jnp.sum(x.reshape(8, 8, 128), axis=0) for t, x in zip(total, terms))
    total = tuple(jnp.zeros((8, 128), f32) for _ in range(6))
    for r in range(4, 12):
        total = sums(r, total)
    row = jnp.zeros((1, 128), f32)
    place = lax.broadcasted_iota(i32, (1, 128), 1)
    for k in range(6):
        row = jnp.where(place == k, jnp.sum(total[k]), row)
    moments[...] = jnp.broadcast_to(row[:, None, :], moments.shape)


def sweeps(refs, packed, edge_0, edge_1):
    padded, plane = pltpu.VMEM((2, 16, 80, 128), f32), pltpu.VMEM((2, 16, 64, 128), f32)
    return pl.pallas_call(
        sweeps_kernel,
        out_shape=(S((3, 10, 64, 128), f32), S((3, 8, 64, 128), f32), S((NGX * NGY, 1, 128), f32)),
        in_specs=[VSPEC] * 8,
        out_specs=(VSPEC,) * 3,
        scratch_shapes=[pltpu.VMEM((3, 2, 16, 80, 128), f32), padded, plane, plane, plane, padded, plane, plane],
        compiler_params=VM,
        name="sweeps",
    )(*refs, packed, edge_0, edge_1)


def coefficients(mu):
    def form(a, b, shift):
        return sum(a[i] * b[j] * mu[i + j + shift] for i in range(len(a)) for j in range(len(b)))
    zero = jnp.zeros_like(mu[0])
    one = jnp.ones_like(mu[0])
    pressure = [zero, zero, zero]
    scaled, direction = [one], [one]
    norm = mu[0]
    for sweep in range(3):
        step = norm / form(direction, direction, 1)
        for i, c in enumerate(direction):
            pressure[i] = pressure[i] + step * c
        if sweep < 2:
            moved = [zero] + direction
            old = scaled + [zero] * (len(moved) - len(scaled))
            scaled = [a - step * b for a, b in zip(old, moved)]
            following = form(scaled, scaled, 0)
            ratio = following / norm
            direction = [a + ratio * b for a, b in zip(scaled, direction + [zero])]
            norm = following
    return pressure


def gradient_kernel(all_moments, core, beside, pressure, table, p):
    summed = jnp.sum(all_moments[...], axis=0)
    coef = coefficients([jnp.broadcast_to(summed[:, k:k + 1], (8, 128)) for k in range(6)])
    coef = [jnp.broadcast_to(c[:1], (64, 128)) for c in coef]
    lane = plane_lanes()
    first, last = lane == 0, lane == 127

    def combine(ref, r):
        return coef[0] * ref[0, r] + coef[1] * ref[1, r] + coef[2] * ref[2, r]
    for r in range(3, 13):
        p[r, 0:8] = jnp.zeros((8, 128), f32)
        p[r, 72:80] = jnp.zeros((8, 128), f32)
        p[r, MID] = combine(core, r - 3)
    for x in range(8):
        r = x + 4
        pair = (p[r, MID], combine(beside, x))
        pressure[pl.ds(x, 64, stride=8), :] = pair[0]
        put_table(table, 0, x, 0.5 * (p[r + 1, MID] - p[r - 1, MID]))
        put_table(table, 1, x, 0.5 * (up_pair(pair, last)[0] - down_pair(pair, first)[0]))
        put_table(table, 2, x, 0.5 * (p[r, UP] - p[r, DOWN]))


def gradients(all_moments, core, beside):
    return pl.pallas_call(
        gradient_kernel,
        out_shape=(S((512, 128), f32), S((NW, 48, 256), bf16)),
        in_specs=[VSPEC] * 3,
        out_specs=(VSPEC,) * 2,
        scratch_shapes=[pltpu.VMEM((16, 80, 128), f32)],
        compiler_params=VM,
        name="gradients",
    )(all_moments, core, beside)


def arrange_kernel(*refs):
    for i, out in enumerate(refs[3:]):
        for d in range(3):
            out[d * PR:(d + 1) * PR, :] = refs[d][i * PR:(i + 1) * PR, :]


def arrange(*arrays):
    return pl.pallas_call(
        arrange_kernel,
        out_shape=(S((3 * PR, 128), f32),) * 5,
        in_specs=[VSPEC] * 3,
        out_specs=(VSPEC,) * 5,
        compiler_params=VM,
        name="arrange",
    )(*arrays)


def place_kernel(back_refs, groups, *refs):
    n = back_refs
    backs, (pos_a, pos_b), out = refs[:n], refs[n:n + 2], refs[n + 2]
    stage, found, tiles, zeros, sem_zero, sem_tile = refs[n + 3:]
    hx, hy = lax.axis_index("gx"), lax.axis_index("gy")
    zeros[...] = jnp.zeros_like(zeros)

    def tile_at(t):
        return out.at[:, 0, pl.ds(pl.multiple_of(t * 8, 8), 8), :]

    def far(t):
        return jnp.abs(t - hx) > 2
    for t in range(16):
        @pl.when(far(t))
        def _():
            pltpu.make_async_copy(zeros, tile_at(t), sem_zero.at[t]).start()
    where = {-2: 0, -1: 1, 0: 2, 1: 3, 2: 4}
    for g, runs in enumerate(groups):
        side = lax.rem(hx // abs(runs[0][0]), 2) == 0
        pair = (backs[0], backs[1]) if g == 0 else (backs[3], backs[4])
        up = lax.rem(hy, 2) == 0
        sources = (jnp.where(up, 2 * PR, 0), PR, jnp.where(up, 0, 2 * PR))
        for ref, first in zip(pair, (jnp.where(side, 3 * PR, 0), jnp.where(side, 0, 3 * PR))):
            for d in range(3):
                to = pl.multiple_of(first + d * PR, 8)
                stage[pl.ds(to, PR), :] = ref[pl.ds(pl.multiple_of(sources[d], 8), PR), :]
        _, dy0, first, count = runs[2]
        for d in range(count):
            src = pl.multiple_of(sources[dy0 + 1 + d], 8)
            stage[(first + d) * PR:(first + d + 1) * PR, :] = backs[2][pl.ds(src, PR), :]
        if g == 1:
            stage[7 * PR:8 * PR, :] = jnp.zeros((PR, 128), f32)
        pos_ref = (pos_a, pos_b)[g]

        def chunk(c):
            k = pos_ref[c]
            at, src = k & 127, k >> 7
            acc = [jnp.zeros((8, 128), f32) for _ in range(3)]
            for v in range(CH):
                here = src == v
                for f in range(3):
                    got = jnp.take_along_axis(stage[pl.ds(f * CH + v, 8, stride=PR), :], at, axis=1)
                    acc[f] = jnp.where(here, got, acc[f])
            for f in range(3):
                found[g, f, c] = acc[f]
        unrolled(CH, 8, chunk)
    row = lax.broadcasted_iota(i32, (8, 128), 0)
    for dx in (-2, -1, 0, 1, 2):
        pieces = [(g, run) for g, runs in enumerate(groups) for run in runs if run[0] == dx]
        turned = []
        for g, (_, dy0, first, count) in pieces:
            shift = lax.rem(hy + dy0 - first + 16, 8)
            low = hy + dy0
            turned.append((g, shift, (row >= low) & (row < low + count)))
        for f in range(3):
            for c in range(CH):
                got = jnp.zeros((8, 128), f32)
                for g, shift, mask in turned:
                    got = jnp.where(mask, pltpu.roll(found[g, f, c], shift, 0), got)
                tiles[where[dx], f, :, c * 128:(c + 1) * 128] = got

        @pl.when((hx + dx >= 0) & (hx + dx < NGX))
        def _():
            pltpu.make_async_copy(tiles.at[where[dx]], tile_at(hx + dx), sem_tile.at[where[dx]]).start()
    for t in range(16):
        @pl.when(far(t))
        def _():
            pltpu.make_async_copy(zeros, tile_at(t), sem_zero.at[t]).wait()
    for dx in (-2, -1, 0, 1, 2):
        @pl.when((hx + dx >= 0) & (hx + dx < NGX))
        def _():
            pltpu.make_async_copy(tiles.at[where[dx]], tile_at(hx + dx), sem_tile.at[where[dx]]).wait()


def place_forces(backs, pos):
    return pl.pallas_call(
        functools.partial(place_kernel, len(backs), GROUPS),
        out_shape=S((3, 1, 128, 3072), f32),
        in_specs=[VSPEC] * (len(backs) + 2),
        out_specs=pl.BlockSpec(memory_space=pl.ANY),
        scratch_shapes=[
            pltpu.VMEM((8 * PR, 128), f32),
            pltpu.VMEM((2, 3, CH, 8, 128), f32),
            pltpu.VMEM((5, 3, 8, 3072), f32),
            pltpu.VMEM((3, 8, 3072), f32),
            pltpu.SemaphoreType.DMA((16,)),
            pltpu.SemaphoreType.DMA((5,)),
        ],
        compiler_params=VM,
        name="place_forces",
    )(*backs, *pos)


def exchange(x, axis, by, which):
    count = {"gx": NGX, "gy": NGY}[axis]
    pairs = [(i, i + by) for i in range(count - by) if (i // by) % 2 == which]
    return lax.ppermute(x, axis, pairs + [(j, i) for i, j in pairs])


def per_device(particle_data, particle_cells, slot_counts, fluid_velocity):
    two_0, two_1, zero_a, keys_a = sort_blocks(GROUPS[0], particle_data, particle_cells, slot_counts)
    two_0, two_1 = exchange(two_0, "gx", 2, 0), exchange(two_1, "gx", 2, 1)
    one_0, one_1, zero_b, keys_b = sort_blocks(GROUPS[1], particle_data, particle_cells, slot_counts)
    one_0, one_1 = exchange(one_0, "gx", 1, 0), exchange(one_1, "gx", 1, 1)
    along = [two_0, two_1, jnp.concatenate([zero_a, zero_b], axis=0), one_0, one_1]
    below, mine, above = [jnp.concatenate([a[d * BR:(d + 1) * BR] for a in along], axis=0) for d in range(3)]
    up = lax.rem(lax.axis_index("gy"), 2) == 0
    sides = [
        exchange(jnp.where(up, above, below), "gy", 1, 0),
        exchange(jnp.where(up, below, above), "gy", 1, 1),
    ]
    bases = tuple(range(0, 5 * BR, BR))
    acc = deposit([mine], bases, 8)
    table, own, send_0, send_1, token = deposit(sides, bases, 4, acc, fluid_velocity.reshape(3, 512, 128))
    rows = (own, send_0, send_1, exchange(send_0, "gx", 1, 0), exchange(send_1, "gx", 1, 1))
    *pos, token = inverse(keys_a, keys_b, token)
    packed = pack_edges(rows, token)
    core, beside, moments = sweeps(rows, packed, exchange(packed, "gy", 1, 0), exchange(packed, "gy", 1, 1))
    everyone = lax.all_to_all(moments, ("gx", "gy"), 0, 0)
    pressure, slopes = gradients(everyone, core, beside)
    far_0, far_1, token = interp(sides, bases, table, slopes, 4, token, 2)
    back = [exchange(far_0, "gy", 1, 0), exchange(far_1, "gy", 1, 1)]
    near, _ = interp([mine], bases, table, slopes, 8, token, 1)
    blocks = list(arrange(back[0], near, back[1]))
    for i, (by, which) in ((0, (2, 0)), (1, (2, 1)), (3, (1, 0)), (4, (1, 1))):
        blocks[i] = exchange(blocks[i], "gx", by, which)
    drag = place_forces(blocks, pos)
    return pressure.reshape(64, 8, 128), drag


def solution(mesh):
    return jax.shard_map(
        per_device,
        mesh=mesh,
        in_specs=(
            P(None, ("gx", "gy"), None, None),
            P(None, ("gx", "gy"), None, None),
            P(("gx", "gy"), None),
            P(None, None, "gx", "gy"),
        ),
        out_specs=(P(None, "gx", "gy"), P(None, ("gx", "gy"), None, None)),
        check_vma=False,
    )
```

```python
import functools
import jax
import jax.numpy as jnp
from jax import lax
from jax.experimental import pallas as pl
from jax.experimental.pallas import tpu as pltpu
from jax.sharding import PartitionSpec as P

f32, bf16, i32 = jnp.float32, jnp.bfloat16, jnp.int32
CH = 24
BR = 152
WL = 16
NW = 32
SPAN = WL * 128
PR = 3 * CH
VM = pltpu.CompilerParams(vmem_limit_bytes=24 * 1024 * 1024)
VSPEC = pl.BlockSpec(memory_space=pltpu.VMEM)
S = jax.ShapeDtypeStruct
TOKEN = S((8, 128), f32)


def sort_network(x):
    lane = lax.broadcasted_iota(i32, (1, 8, 128), 2)
    flipped = None
    for merge in range(1, 13):
        if merge < 12:
            if merge >= 5:
                want = (lane >> (merge - 5)) & 1
                mask = -want
            else:
                mask = jnp.asarray(-((lax.broadcasted_iota(i32, (32, 8, 128), 0) >> merge) & 1))
        else:
            mask = None
        if mask is not None:
            x = x ^ mask
        for bit in range(merge - 1, -1, -1):
            if bit < 5:
                step = 1 << bit
                y = x.reshape(32 // (2 * step), 2, step, 8, 128)
                a, b = y[:, 0], y[:, 1]
                x = jnp.stack([jnp.minimum(a, b), jnp.maximum(a, b)], axis=1).reshape(32, 8, 128)
            else:
                step = 1 << (bit - 5)
                up = (lane & step) != 0
                other = jnp.take_along_axis(x, jnp.broadcast_to(lane ^ step, x.shape), axis=2)
                x = jnp.where(up, jnp.maximum(x, other), jnp.minimum(x, other))
        if mask is not None:
            x = x ^ mask
    return x


def lanes_to_chunks(x):
    lane = lax.broadcasted_iota(i32, (1, 8, 128), 2)
    for bit in range(5):
        step = 1 << bit
        y = x.reshape(32 // (2 * step), 2, step, 8, 128)
        a, b = y[:, 0], y[:, 1]
        up = ((lane & step) != 0)[:, None]
        na = jnp.where(up, pltpu.roll(b, step, 3), a)
        nb = jnp.where(up, b, pltpu.roll(a, 128 - step, 3))
        x = jnp.stack([na, nb], axis=1).reshape(32, 8, 128)
    for bit in range(2):
        step, far = 1 << bit, 32 << bit
        y = x.reshape(32 // (2 * step), 2, step, 8, 128)
        a, b = y[:, 0], y[:, 1]
        up = ((lane & far) != 0)[:, None]
        na = jnp.where(up, pltpu.roll(b, far, 3), a)
        nb = jnp.where(up, b, pltpu.roll(a, 128 - far, 3))
        x = jnp.stack([na, nb], axis=1).reshape(32, 8, 128)
    return jnp.stack([x[(c % 8) * 4 + c // 8] for c in range(32)], axis=0)


GROUPS = (((-2, -1, 0, 3), (2, -1, 3, 3), (0, -1, 6, 2)), ((-1, -1, 0, 3), (1, -1, 3, 3), (0, 1, 6, 1)))
NGX, NGY = 16, 8


def unrolled(count, by, body):
    def several(i, _):
        for j in range(by):
            body(i * by + j)
        return 0
    lax.fori_loop(0, count // by, several, 0)


def row_mask(first, count):
    row = lax.broadcasted_iota(i32, (8, 128), 0)
    return (row >= first) & (row < first + count)


def sort_kernel(runs, n_out, data_ref, cells_ref, counts_ref, *rest):
    outs, pos_ref = rest[:n_out], rest[n_out]
    data_v, cells_v, key_s, pay_s, out_s, sems = rest[n_out + 1:]
    hx, hy = lax.axis_index("gx"), lax.axis_index("gy")
    copies = []
    for t, (dx, _, _, _) in enumerate(runs):
        tile = pl.ds(pl.multiple_of(jnp.clip(hx + dx, 0, NGX - 1) * 8, 8), 8)
        copies.append(pltpu.make_async_copy(cells_ref.at[:, 0, tile, :], cells_v.at[t], sems.at[2 * t]))
    for t, (dx, _, _, _) in enumerate(runs):
        tile = pl.ds(pl.multiple_of(jnp.clip(hx + dx, 0, NGX - 1) * 8, 8), 8)
        copies.append(pltpu.make_async_copy(data_ref.at[:, 0, tile, :], data_v.at[t], sems.at[2 * t + 1]))
    for copy in copies:
        copy.start()
    lane = lax.broadcasted_iota(i32, (8, 128), 1)
    row = lax.broadcasted_iota(i32, (8, 128), 0)
    counts = jnp.zeros((8, 128), i32)
    for dx, dy0, first, count in runs:
        for i in range(count):
            bx, by = hx + dx, hy + dy0 + i
            valid = (bx >= 0) & (bx < NGX) & (by >= 0) & (by < NGY)
            n = counts_ref[0, jnp.clip(bx * NGY + by, 0, NGX * NGY - 1)]
            counts = jnp.where(row == first + i, jnp.where(valid, n, 0), counts)
    shifts = [lax.rem(first - (hy + dy0) + 16, 8) for _, dy0, first, _ in runs]
    masks = [row_mask(first, count) for _, _, first, count in runs]
    for copy in copies[:len(runs)]:
        copy.wait()

    def gathered(ref, f, c):
        got = None
        for t in range(len(runs)):
            x = pltpu.roll(ref[t, f, :, c * 128:(c + 1) * 128], shifts[t], 0)
            got = x if got is None else jnp.where(masks[t], x, got)
        return got

    rows = []
    for c in range(32):
        slot = lane + c * 128
        if c < CH:
            h, col = gathered(cells_v, 0, c), gathered(cells_v, 1, c)
            live = slot < counts
            cell = (((col >> 7) * 64 + h) << 7) + (col & 127)
            cell = jnp.where(live, cell, 65536)
            rows.append((cell << 12) + slot)
        else:
            rows.append((1 << 29) + slot)
    keys = lanes_to_chunks(sort_network(jnp.stack(rows, axis=0)))
    key_s[...] = keys[:CH]
    pos_ref[...] = keys[:CH]
    for copy in copies[len(runs):]:
        copy.wait()
    for c in range(CH):
        for f in range(5):
            pay_s[f, c] = jnp.where(lane + c * 128 < counts, gathered(data_v, f, c), 0.0)

    def chunk(c):
        k = key_s[c]
        slot = k & 4095
        at, src = slot & 127, slot >> 7
        acc = [jnp.zeros((8, 128), f32) for _ in range(5)]
        for v in range(CH):
            here = src == v
            for f in range(5):
                got = jnp.take_along_axis(pay_s[f, v], at, axis=1)
                acc[f] = jnp.where(here, got, acc[f])
        for f in range(5):
            out_s[pl.ds(f * CH + c, 8, stride=BR), :] = acc[f]
        out_s[pl.ds(5 * CH + c, 8, stride=BR), :] = (k >> 12).astype(f32)
    unrolled(CH, 12, chunk)
    low = lane < 64
    bound = jnp.where(low, lane, lane - 63) * SPAN
    total = jnp.zeros((8, 128), i32)
    for c in range(CH):
        cell = key_s[c] >> 12
        last = jnp.broadcast_to(cell[:, 127:128], (8, 128))
        start = jnp.broadcast_to(cell[:, 0:1], (8, 128))
        total = total + jnp.where(jnp.where(low, last, start) < bound, 1, 0)
    for r in range(8):
        out_s[pl.ds(6 * CH + r, 8, stride=BR), :] = total.astype(f32)
    side = lax.rem(hx // abs(runs[0][0]), 2) == 0
    for out, first in ((outs[0], jnp.where(side, 3 * BR, 0)), (outs[1], jnp.where(side, 0, 3 * BR))):
        out[...] = out_s[pl.ds(pl.multiple_of(first, 8), 3 * BR), :]
    _, _, first, count = runs[2]
    outs[2][...] = out_s[first * BR:(first + count) * BR, :]


def inverse_kernel(keys_a, keys_b, after, pos_a, pos_b, token):
    token[...] = after[...]
    place = lax.broadcasted_iota(i32, (CH, 8, 128), 0) * 128 + lax.broadcasted_iota(i32, (CH, 8, 128), 2)
    rest = jnp.full((32 - CH, 8, 128), 1 << 29, i32)
    for keys, pos in ((keys_a, pos_a), (keys_b, pos_b)):
        back = jnp.concatenate([((keys[...] & 4095) << 12) + place, rest], axis=0)
        pos[...] = lanes_to_chunks(sort_network(back))[:CH] & 4095


def inverse(keys_a, keys_b, after):
    shape = jax.ShapeDtypeStruct((CH, 8, 128), i32)
    return pl.pallas_call(
        inverse_kernel,
        out_shape=(shape, shape, TOKEN),
        in_specs=[VSPEC] * 3,
        out_specs=(VSPEC,) * 3,
        compiler_params=VM,
        cost_estimate=pl.CostEstimate(flops=10**9, bytes_accessed=2 * 10**7, transcendentals=0),
        name="inverse",
    )(keys_a, keys_b, after)


def sort_blocks(runs, data, cells, counts):
    shapes = [jax.ShapeDtypeStruct((count * BR, 128), f32) for _, _, _, count in runs]
    shapes.append(jax.ShapeDtypeStruct((CH, 8, 128), i32))
    n = len(runs)
    return pl.pallas_call(
        functools.partial(sort_kernel, runs, n),
        out_shape=tuple(shapes),
        in_specs=[pl.BlockSpec(memory_space=pltpu.HBM)] * 2 + [pl.BlockSpec(memory_space=pltpu.SMEM)],
        out_specs=(pl.BlockSpec(memory_space=pltpu.VMEM),) * (n + 1),
        scratch_shapes=[
            pltpu.VMEM((n, 5, 8, 3072), f32),
            pltpu.VMEM((n, 2, 8, 3072), i32),
            pltpu.VMEM((CH, 8, 128), i32),
            pltpu.VMEM((5, CH, 8, 128), f32),
            pltpu.VMEM((8 * BR, 128), f32),
            pltpu.SemaphoreType.DMA((2 * n,)),
        ],
        compiler_params=pltpu.CompilerParams(vmem_limit_bytes=50 * 1024 * 1024),
        name="sort_blocks",
    )(data, cells, counts)


def load_offsets(refs, off_v, off_s, sem):
    for j, (ref, base) in enumerate(refs):
        off_v[j:j + 1, :] = ref[base + 6 * CH:base + 6 * CH + 1, :].astype(i32)
    copy = pltpu.make_async_copy(off_v, off_s, sem)
    copy.start()
    copy.wait()


def wide(row, rows):
    return jnp.broadcast_to(row, (rows, 128))


def split_cell(cell):
    line = jnp.floor(cell * (1.0 / 128.0))
    return line, cell - line * 128.0


def width_onehot(wid, iota):
    w16 = wide(wid, 16).astype(bf16)
    w = jnp.concatenate([w16] * 8, axis=0)
    return jnp.where(w == iota, jnp.asarray(1.0, bf16), jnp.asarray(0.0, bf16))


def deposit_kernel(nref, bases, unroll, use_acc, *refs):
    blocks = [(refs[i], b) for i in range(nref) for b in bases]
    nb = len(blocks)
    rest = refs[nref:]
    if use_acc:
        prev, fluid, table, own, send_0, send_1, token, out, flux, pre, off_v, off_s, sem = rest
    else:
        out, pre, off_v, off_s, sem = rest
    load_offsets(blocks, off_v, off_s, sem)
    for j, (ref, base) in enumerate(blocks):
        vol = ref[base:base + CH, :]
        coef = ref[base + CH:base + 2 * CH, :]
        vals = [vol, coef] + [coef * ref[base + (2 + d) * CH:base + (3 + d) * CH, :] for d in range(3)]
        for k, v in enumerate(vals):
            hi = v.astype(bf16).astype(f32)
            pre[j, k] = hi
            pre[j, 5 + k] = v - hi
        line, wid = split_cell(ref[base + 5 * CH:base + 6 * CH, :])
        pre[j, 10] = line
        pre[j, 11] = wid
    iota = lax.broadcasted_iota(i32, (128, 128), 0).astype(f32).astype(bf16)
    iota16 = lax.broadcasted_iota(i32, (16, 128), 0).astype(f32).astype(bf16)
    zero = jnp.zeros((16, 128), bf16)

    def operands(j, c, w):
        rel = jnp.clip(pre[j, 10, pl.ds(c, 1), :] - (w * WL).astype(f32), -1.0, 16.0)
        mask = wide(rel, 16).astype(bf16) == iota16
        a = jnp.concatenate(
            [jnp.where(mask, wide(pre[j, k, pl.ds(c, 1), :], 16).astype(bf16), zero) for k in range(10)], axis=0)
        return a, width_onehot(pre[j, 11, pl.ds(c, 1), :], iota)

    def product(a, b):
        p = lax.dot_general(a, b, (((1,), (1,)), ((), ())), preferred_element_type=f32)
        return p

    def halves(p):
        return (p[:80] + p[80:]).reshape(5, WL, 128)

    def windows(i, more):
        for u in range(unroll):
            w = i * unroll + u
            total = None
            for j in range(nb):
                first = jnp.minimum(off_s[j, w], CH - 2)
                more = jnp.maximum(more, off_s[j, 64 + w] - first)
                a0, b0 = operands(j, first, w)
                a1, b1 = operands(j, first + 1, w)
                p = product(jnp.concatenate([a0, a1], axis=1), jnp.concatenate([b0, b1], axis=1))
                total = p if total is None else total + p
            total = halves(total)
            rows = pl.ds(pl.multiple_of(w * WL, WL), WL)
            if use_acc:
                total = total + prev[:, rows, :]
            out[:, rows, :] = total
        return more
    more = lax.fori_loop(0, NW // unroll, windows, jnp.int32(0))

    @pl.when(more > 2)
    def _():
        def window(w, _):
            rows = pl.ds(pl.multiple_of(w * WL, WL), WL)

            def block(j, _):
                def step(c, _):
                    a, b = operands(j, c, w)
                    out[:, rows, :] += halves(product(a, b))
                    return 0
                return lax.fori_loop(jnp.minimum(off_s[j, w], CH - 2) + 2, off_s[j, 64 + w], step, 0)
            return lax.fori_loop(0, nb, block, 0)
        lax.fori_loop(0, NW, window, 0)


    if use_acc:
        fields(out, fluid, table, own, send_0, send_1, flux)
        token[...] = jnp.zeros_like(token)


def deposit(arrays, bases, unroll, prev=None, fluid=None):
    nb = len(arrays) * len(bases)
    args = list(arrays) + ([] if prev is None else [prev, fluid])
    total = S((5, 512, 128), f32)
    sent = S((SENT, 64, 128), f32)
    shapes = (S((NW, 48, 256), bf16), S((2, 8, 64, 128), f32), sent, sent, TOKEN)
    scratch = [
        pltpu.VMEM((nb, 12, CH, 128), f32),
        pltpu.VMEM((nb, 128), i32),
        pltpu.SMEM((nb, 128), i32),
        pltpu.SemaphoreType.DMA,
    ]
    if prev is not None:
        scratch = [pltpu.VMEM((5, 512, 128), f32), pltpu.VMEM((8, 64, 128), f32)] + scratch
    return pl.pallas_call(
        functools.partial(deposit_kernel, len(arrays), bases, unroll, prev is not None),
        out_shape=total if prev is None else shapes,
        in_specs=[VSPEC] * len(args),
        out_specs=VSPEC if prev is None else (VSPEC,) * 5,
        scratch_shapes=scratch,
        compiler_params=VM,
        cost_estimate=pl.CostEstimate(flops=10**9 * nb, bytes_accessed=3 * 10**6 * nb, transcendentals=0),
        name="deposit",
    )(*args)


def interp_kernel(nref, bases, unroll, *refs):
    blocks = [(refs[i], b) for i in range(nref) for b in bases]
    nb = len(blocks)
    fast, slope, _ = refs[nref:nref + 3]
    outs = refs[nref + 3:-6]
    token, pre, acc, off_v, off_s, sem = refs[-6:]
    each = nb // len(outs)
    token[...] = jnp.zeros_like(token)
    load_offsets(blocks, off_v, off_s, sem)
    for j, (ref, base) in enumerate(blocks):
        line, wid = split_cell(ref[base + 5 * CH:base + 6 * CH, :])
        pre[j, 0] = line
        pre[j, 1] = wid
        pre[j, 2] = ref[base + CH:base + 2 * CH, :]
        pre[j, 3] = -ref[base:base + CH, :]
    acc[...] = jnp.zeros_like(acc)
    iota = lax.broadcasted_iota(i32, (128, 128), 0).astype(f32).astype(bf16)
    iota16 = lax.broadcasted_iota(i32, (16, 128), 0).astype(f32)

    def visit(j, c, w, width, tab):
        scales, hots = [], []
        for i in range(width):
            at = pl.ds(c + i, 1)
            mask = wide(pre[j, 0, at, :] - (w * WL).astype(f32), 16) == iota16
            scales.append([jnp.where(mask, wide(pre[j, 2 + s, at, :], 16), 0.0) for s in range(2)])
            b = width_onehot(pre[j, 1, at, :], iota)
            hots.append(jnp.concatenate([b, b], axis=0))
        hot = hots[0] if width == 1 else jnp.concatenate(hots, axis=1)
        g = jnp.dot(tab, hot, preferred_element_type=f32)
        for i in range(width):
            for k in range(3):
                lanes = slice(i * 128, (i + 1) * 128)
                part = scales[i][0] * g[k * 16:k * 16 + 16, lanes]
                part = part + scales[i][1] * g[48 + k * 16:64 + k * 16, lanes]
                acc[j, c + i, k] += part[:8] + part[8:]

    def windows(i, more):
        for u in range(unroll):
            w = i * unroll + u
            tab = jnp.concatenate([fast[w], slope[w]], axis=0)
            for j in range(nb):
                first = jnp.minimum(off_s[j, w], CH - 2)
                more = jnp.maximum(more, off_s[j, 64 + w] - first)
                visit(j, first, w, 2, tab)
        return more
    more = lax.fori_loop(0, NW // unroll, windows, jnp.int32(0))

    @pl.when(more > 2)
    def _():
        def window(w, _):
            tab = jnp.concatenate([fast[w], slope[w]], axis=0)

            def block(j, _):
                def step(c, _):
                    visit(j, c, w, 1, tab)
                    return 0
                return lax.fori_loop(jnp.minimum(off_s[j, w], CH - 2) + 2, off_s[j, 64 + w], step, 0)
            return lax.fori_loop(0, nb, block, 0)
        lax.fori_loop(0, NW, window, 0)
    for j, (ref, base) in enumerate(blocks):
        coef = ref[base + CH:base + 2 * CH, :]
        for k in range(3):
            vel = ref[base + (2 + k) * CH:base + (3 + k) * CH, :]
            at = (j % each) * PR + k * CH
            outs[j // each][at:at + CH, :] = jnp.sum(acc[j, :, k], axis=1) - coef * vel


def interp(arrays, bases, fast, slope, unroll, after, n_out):
    nb = len(arrays) * len(bases)
    args = list(arrays) + [fast, slope, after]
    return pl.pallas_call(
        functools.partial(interp_kernel, len(arrays), bases, unroll),
        out_shape=(S((nb // n_out * PR, 128), f32),) * n_out + (TOKEN,),
        in_specs=[VSPEC] * len(args),
        out_specs=(VSPEC,) * (n_out + 1),
        scratch_shapes=[
            pltpu.VMEM((nb, 4, CH, 128), f32),
            pltpu.VMEM((nb, CH, 3, 8, 128), f32),
            pltpu.VMEM((nb, 128), i32),
            pltpu.SMEM((nb, 128), i32),
            pltpu.SemaphoreType.DMA,
        ],
        compiler_params=VM,
        cost_estimate=pl.CostEstimate(flops=10**9 * nb, bytes_accessed=3 * 10**6 * nb, transcendentals=0),
        name="interp",
    )(*args)

TIME_STEP = 0.1
SHIFT = 0.05


def put_table(table, k, x, values):
    hi = values.astype(bf16)
    lo = (values - hi.astype(f32)).astype(bf16)
    for q in range(4):
        table[4 * x + q, k * 16:k * 16 + 16, 0:128] = hi[16 * q:16 * q + 16]
        table[4 * x + q, k * 16:k * 16 + 16, 128:256] = lo[16 * q:16 * q + 16]


def up_z(x):
    return jnp.concatenate([x[1:], jnp.zeros_like(x[:1])], axis=0)


def down_z(x):
    return jnp.concatenate([jnp.zeros_like(x[:1]), x[:-1]], axis=0)


def plane_lanes():
    return lax.broadcasted_iota(i32, (64, 128), 1)


def is_even(axis):
    return lax.rem(lax.axis_index(axis), 2) == 0


def turn(x, by):
    return x if by % 128 == 0 else pltpu.roll(x, by % 128, 1)


SENT = 9


def fields(acc, fluid, table, own, send_0, send_1, flux):
    even = is_even("gx")
    lane = plane_lanes()
    ends = jnp.zeros((64, 128), f32)
    for x in range(8):
        at = slice(x * 64, x * 64 + 64)
        fraction = acc[0, at, :]
        drag = acc[1, at, :]
        porosity = 1.0 / (1.0 + fraction)
        fluxes = []
        for d in range(3):
            fluid_d = fluid[d, pl.ds(x, 64, stride=8), :]
            predicted = fluid_d + TIME_STEP * (1.0 + fraction) * (acc[2 + d, at, :] - drag * fluid_d)
            put_table(table, d, x, predicted)
            fluxes.append(porosity * predicted)
        flux[x] = fluxes[0]
        fy, fz = fluxes[1:]
        along_y = jnp.where(lane < 127, turn(fy, -1), 0.0) - jnp.where(lane > 0, turn(fy, 1), 0.0)
        own[0, x] = porosity
        own[1, x] = -0.5 * (along_y + (up_z(fz) - down_z(fz)))
        mid = 8 * (x + 4)
        ends = jnp.where((lane == mid) | (lane == mid - 1), turn(fy, mid), ends)
    for x in range(8):
        along_x = (flux[x + 1] if x < 7 else 0.0) - (flux[x - 1] if x > 0 else 0.0)
        own[1, x] = own[1, x] - 0.5 * along_x
    low = [own[0, x] for x in range(4)] + [own[1, x] for x in range(3)] + [flux[0], ends]
    high = [own[0, x] for x in range(4, 8)] + [own[1, x] for x in range(5, 8)] + [flux[7], ends]
    for i in range(SENT):
        send_0[i] = jnp.where(even, high[i], low[i])
        send_1[i] = jnp.where(even, low[i], high[i])


def extended(refs):
    own, sent_0, sent_1, got_0, got_1 = refs
    even = is_even("gx")

    def below(i):
        return jnp.where(even, got_1[i], got_0[i])

    def above(i):
        return jnp.where(even, got_0[i], got_1[i])

    def porosity(r):
        return below(r) if r < 4 else own[0, r - 4] if r < 12 else above(r - 12)

    def source(r):
        if r == 3:
            return below(6) - 0.5 * jnp.where(even, sent_1[7], sent_0[7])
        if r == 4:
            return own[1, 0] + 0.5 * below(7)
        if r == 11:
            return own[1, 7] - 0.5 * above(7)
        if r == 12:
            return above(4) + 0.5 * jnp.where(even, sent_0[7], sent_1[7])
        return below(3 + r) if r < 4 else own[1, r - 4] if r < 12 else above(r - 8)

    def ends():
        lane = plane_lanes()
        beside = jnp.where((lane >= 92) & (lane < 124), turn(above(8), 64), turn(below(8), 64))
        return jnp.where((lane >= 28) & (lane < 92), sent_0[8], beside)
    return porosity, source, ends


def pack_kernel(own, sent_0, sent_1, got_0, got_1, after, out):
    del after
    porosity, source, ends = extended((own, sent_0, sent_1, got_0, got_1))
    lane = plane_lanes()
    for f, (rows, get) in enumerate(((range(16), porosity), (range(1, 15), source))):
        got = jnp.zeros((64, 128), f32)
        for r in rows:
            place = (lax.rem(lane + 132 - 8 * r, 128)) < 8
            got = jnp.where(place, turn(get(r), 8 * r), got)
        out[f] = got
    out[2] = ends()


def pack_edges(refs, after):
    return pl.pallas_call(
        pack_kernel,
        out_shape=S((3, 64, 128), f32),
        in_specs=[VSPEC] * 6,
        out_specs=VSPEC,
        compiler_params=VM,
        name="pack_edges",
    )(*refs, after)


def face(e, n):
    return 2.0 * e * n / jnp.maximum(e + n, 1e-30)


def up_pair(pair, last):
    a, b = (pltpu.roll(x, 127, 1) for x in pair)
    return jnp.where(last, b, a), jnp.where(last, a, b)


def down_pair(pair, first):
    a, b = (pltpu.roll(x, 1, 1) for x in pair)
    return jnp.where(first, b, a), jnp.where(first, a, b)


MID, UP, DOWN = pl.ds(8, 64), pl.ds(9, 64), pl.ds(7, 64)


def sweeps_kernel(own, sent_0, sent_1, got_0, got_1, packed, edge_0, edge_1, core, beside, moments, vs, por, src, wx, wy, wz,
                  diag, inv):
    porosity, source, _ = extended((own, sent_0, sent_1, got_0, got_1))
    lane = plane_lanes()
    first, last = lane == 0, lane == 127
    keep = (lane < 4) | (lane >= 124)
    even_y = is_even("gy")

    def above(f):
        return jnp.where(even_y, edge_0[f], edge_1[f])

    def below(f):
        return jnp.where(even_y, edge_1[f], edge_0[f])
    part = lane & 7

    def crossed(from_below, from_above):
        return jnp.where(part == 0, 0.5 * turn(from_below, 1), jnp.where(part == 7, -0.5 * turn(from_above, -1), 0.0))
    side_e = jnp.where(part < 4, above(0), below(0))
    side_b = jnp.where(part < 4, above(1), below(1)) + crossed(packed[2], packed[2])
    core_b = crossed(below(2), above(2))
    for ref in (por, wz):
        for h in range(2):
            for r in range(16):
                ref[h, r, 0:8] = jnp.zeros((8, 128), f32)
                ref[h, r, 72:80] = jnp.zeros((8, 128), f32)
    for k in range(3):
        for r in range(1, 15):
            for h in range(2):
                vs[k, h, r, 0:8] = jnp.zeros((8, 128), f32)
                vs[k, h, r, 72:80] = jnp.zeros((8, 128), f32)
    for r in range(16):
        por[0, r, MID] = porosity(r)
        por[1, r, MID] = jnp.where(keep, turn(side_e, -8 * r), 0.0)
        if 0 < r < 15:
            src[0, r] = source(r) + jnp.where(first | last, turn(core_b, -8 * r), 0.0)
            src[1, r] = jnp.where(keep, turn(side_b, -8 * r), 0.0)

    def faces(r):
        pair = [por[h, r, MID] for h in range(2)]
        up = up_pair(pair, last)
        for h in range(2):
            wx[h, r] = face(pair[h], por[h, r + 1, MID])
            wy[h, r] = face(pair[h], up[h])
            wz[h, r, MID] = face(pair[h], por[h, r, UP])
    for r in range(15):
        faces(r)

    def keep_plane(k, h, r, v):
        vs[k, h, r, MID] = v
        if h == 0 and 3 <= r < 13:
            core[k, r - 3] = v
        if h == 1 and 4 <= r < 12:
            beside[k, r - 4] = v

    def sources(r):
        y = [wy[h, r] for h in range(2)]
        y_down = down_pair(y, first)
        for h in range(2):
            e = por[h, r, MID]
            d = SHIFT * e + wx[h, r] + wx[h, r - 1] + y[h] + y_down[h] + wz[h, r, MID] + wz[h, r, DOWN]
            outside = e == 0.0
            i = jnp.where(outside, 0.0, 1.0 / jnp.where(outside, 1.0, d))
            diag[h, r] = d
            inv[h, r] = i
            keep_plane(0, h, r, src[h, r] * i)
    for r in range(1, 15):
        sources(r)

    def spread(k, r, halves):
        pair = [vs[k, h, r, MID] for h in range(2)]
        y = [wy[h, r] for h in range(2)]
        up = up_pair(pair, last)
        down = down_pair([a * b for a, b in zip(y, pair)], first)
        made = []
        for h in range(halves):
            total = wx[h, r] * vs[k, h, r + 1, MID] + wx[h, r - 1] * vs[k, h, r - 1, MID]
            total = total + y[h] * up[h] + down[h]
            total = total + wz[h, r, MID] * vs[k, h, r, UP] + wz[h, r, DOWN] * vs[k, h, r, DOWN]
            made.append((diag[h, r] * pair[h] - total) * inv[h, r])
        return made

    for k, (lo, hi) in ((0, (2, 14)), (1, (3, 13))):
        for r in range(lo, hi):
            for h, v in enumerate(spread(k, r, 2)):
                keep_plane(k + 1, h, r, v)

    def sums(r, total):
        d = diag[0, r]
        v0, v1, v2 = (vs[k, 0, r, MID] for k in range(3))
        v3, = spread(2, r, 1)
        d0, d1, d2 = d * v0, d * v1, d * v2
        terms = (d0 * v0, d0 * v1, d1 * v1, d1 * v2, d2 * v2, d2 * v3)
        return tuple(t + jnp.sum(x.reshape(8, 8, 128), axis=0) for t, x in zip(total, terms))
    total = tuple(jnp.zeros((8, 128), f32) for _ in range(6))
    for r in range(4, 12):
        total = sums(r, total)
    row = jnp.zeros((1, 128), f32)
    place = lax.broadcasted_iota(i32, (1, 128), 1)
    for k in range(6):
        row = jnp.where(place == k, jnp.sum(total[k]), row)
    moments[...] = jnp.broadcast_to(row[:, None, :], moments.shape)


def sweeps(refs, packed, edge_0, edge_1):
    padded, plane = pltpu.VMEM((2, 16, 80, 128), f32), pltpu.VMEM((2, 16, 64, 128), f32)
    return pl.pallas_call(
        sweeps_kernel,
        out_shape=(S((3, 10, 64, 128), f32), S((3, 8, 64, 128), f32), S((NGX * NGY, 1, 128), f32)),
        in_specs=[VSPEC] * 8,
        out_specs=(VSPEC,) * 3,
        scratch_shapes=[pltpu.VMEM((3, 2, 16, 80, 128), f32), padded, plane, plane, plane, padded, plane, plane],
        compiler_params=VM,
        name="sweeps",
    )(*refs, packed, edge_0, edge_1)


def coefficients(mu):
    def form(a, b, shift):
        return sum(a[i] * b[j] * mu[i + j + shift] for i in range(len(a)) for j in range(len(b)))
    zero = jnp.zeros_like(mu[0])
    one = jnp.ones_like(mu[0])
    pressure = [zero, zero, zero]
    scaled, direction = [one], [one]
    norm = mu[0]
    for sweep in range(3):
        step = norm / form(direction, direction, 1)
        for i, c in enumerate(direction):
            pressure[i] = pressure[i] + step * c
        if sweep < 2:
            moved = [zero] + direction
            old = scaled + [zero] * (len(moved) - len(scaled))
            scaled = [a - step * b for a, b in zip(old, moved)]
            following = form(scaled, scaled, 0)
            ratio = following / norm
            direction = [a + ratio * b for a, b in zip(scaled, direction + [zero])]
            norm = following
    return pressure


def gradient_kernel(all_moments, core, beside, pressure, table, p):
    summed = jnp.sum(all_moments[...], axis=0)
    coef = coefficients([jnp.broadcast_to(summed[:, k:k + 1], (8, 128)) for k in range(6)])
    coef = [jnp.broadcast_to(c[:1], (64, 128)) for c in coef]
    lane = plane_lanes()
    first, last = lane == 0, lane == 127

    def combine(ref, r):
        return coef[0] * ref[0, r] + coef[1] * ref[1, r] + coef[2] * ref[2, r]
    for r in range(3, 13):
        p[r, 0:8] = jnp.zeros((8, 128), f32)
        p[r, 72:80] = jnp.zeros((8, 128), f32)
        p[r, MID] = combine(core, r - 3)
    for x in range(8):
        r = x + 4
        pair = (p[r, MID], combine(beside, x))
        pressure[pl.ds(x, 64, stride=8), :] = pair[0]
        put_table(table, 0, x, 0.5 * (p[r + 1, MID] - p[r - 1, MID]))
        put_table(table, 1, x, 0.5 * (up_pair(pair, last)[0] - down_pair(pair, first)[0]))
        put_table(table, 2, x, 0.5 * (p[r, UP] - p[r, DOWN]))


def gradients(all_moments, core, beside):
    return pl.pallas_call(
        gradient_kernel,
        out_shape=(S((512, 128), f32), S((NW, 48, 256), bf16)),
        in_specs=[VSPEC] * 3,
        out_specs=(VSPEC,) * 2,
        scratch_shapes=[pltpu.VMEM((16, 80, 128), f32)],
        compiler_params=VM,
        name="gradients",
    )(all_moments, core, beside)


def arrange_kernel(*refs):
    for i, out in enumerate(refs[3:]):
        for d in range(3):
            out[d * PR:(d + 1) * PR, :] = refs[d][i * PR:(i + 1) * PR, :]


def arrange(*arrays):
    return pl.pallas_call(
        arrange_kernel,
        out_shape=(S((3 * PR, 128), f32),) * 5,
        in_specs=[VSPEC] * 3,
        out_specs=(VSPEC,) * 5,
        compiler_params=VM,
        name="arrange",
    )(*arrays)


def place_kernel(back_refs, groups, *refs):
    n = back_refs
    backs, (pos_a, pos_b), out = refs[:n], refs[n:n + 2], refs[n + 2]
    stage, found, tiles, zeros, sem_zero, sem_tile = refs[n + 3:]
    hx, hy = lax.axis_index("gx"), lax.axis_index("gy")
    zeros[...] = jnp.zeros_like(zeros)

    def tile_at(t):
        return out.at[:, 0, pl.ds(pl.multiple_of(t * 8, 8), 8), :]

    def far(t):
        return jnp.abs(t - hx) > 2
    for t in range(16):
        @pl.when(far(t))
        def _():
            pltpu.make_async_copy(zeros, tile_at(t), sem_zero.at[t]).start()
    where = {-2: 0, -1: 1, 0: 2, 1: 3, 2: 4}
    for g, runs in enumerate(groups):
        side = lax.rem(hx // abs(runs[0][0]), 2) == 0
        pair = (backs[0], backs[1]) if g == 0 else (backs[3], backs[4])
        up = lax.rem(hy, 2) == 0
        sources = (jnp.where(up, 2 * PR, 0), PR, jnp.where(up, 0, 2 * PR))
        for ref, first in zip(pair, (jnp.where(side, 3 * PR, 0), jnp.where(side, 0, 3 * PR))):
            for d in range(3):
                to = pl.multiple_of(first + d * PR, 8)
                stage[pl.ds(to, PR), :] = ref[pl.ds(pl.multiple_of(sources[d], 8), PR), :]
        _, dy0, first, count = runs[2]
        for d in range(count):
            src = pl.multiple_of(sources[dy0 + 1 + d], 8)
            stage[(first + d) * PR:(first + d + 1) * PR, :] = backs[2][pl.ds(src, PR), :]
        if g == 1:
            stage[7 * PR:8 * PR, :] = jnp.zeros((PR, 128), f32)
        pos_ref = (pos_a, pos_b)[g]

        def chunk(c):
            k = pos_ref[c]
            at, src = k & 127, k >> 7
            acc = [jnp.zeros((8, 128), f32) for _ in range(3)]
            for v in range(CH):
                here = src == v
                for f in range(3):
                    got = jnp.take_along_axis(stage[pl.ds(f * CH + v, 8, stride=PR), :], at, axis=1)
                    acc[f] = jnp.where(here, got, acc[f])
            for f in range(3):
                found[g, f, c] = acc[f]
        unrolled(CH, 24, chunk)
    row = lax.broadcasted_iota(i32, (8, 128), 0)
    for dx in (-2, -1, 0, 1, 2):
        pieces = [(g, run) for g, runs in enumerate(groups) for run in runs if run[0] == dx]
        turned = []
        for g, (_, dy0, first, count) in pieces:
            shift = lax.rem(hy + dy0 - first + 16, 8)
            low = hy + dy0
            turned.append((g, shift, (row >= low) & (row < low + count)))
        for f in range(3):
            for c in range(CH):
                got = jnp.zeros((8, 128), f32)
                for g, shift, mask in turned:
                    got = jnp.where(mask, pltpu.roll(found[g, f, c], shift, 0), got)
                tiles[where[dx], f, :, c * 128:(c + 1) * 128] = got

        @pl.when((hx + dx >= 0) & (hx + dx < NGX))
        def _():
            pltpu.make_async_copy(tiles.at[where[dx]], tile_at(hx + dx), sem_tile.at[where[dx]]).start()
    for t in range(16):
        @pl.when(far(t))
        def _():
            pltpu.make_async_copy(zeros, tile_at(t), sem_zero.at[t]).wait()
    for dx in (-2, -1, 0, 1, 2):
        @pl.when((hx + dx >= 0) & (hx + dx < NGX))
        def _():
            pltpu.make_async_copy(tiles.at[where[dx]], tile_at(hx + dx), sem_tile.at[where[dx]]).wait()


def place_forces(backs, pos):
    return pl.pallas_call(
        functools.partial(place_kernel, len(backs), GROUPS),
        out_shape=S((3, 1, 128, 3072), f32),
        in_specs=[VSPEC] * (len(backs) + 2),
        out_specs=pl.BlockSpec(memory_space=pl.ANY),
        scratch_shapes=[
            pltpu.VMEM((8 * PR, 128), f32),
            pltpu.VMEM((2, 3, CH, 8, 128), f32),
            pltpu.VMEM((5, 3, 8, 3072), f32),
            pltpu.VMEM((3, 8, 3072), f32),
            pltpu.SemaphoreType.DMA((16,)),
            pltpu.SemaphoreType.DMA((5,)),
        ],
        compiler_params=VM,
        name="place_forces",
    )(*backs, *pos)


def exchange(x, axis, by, which):
    count = {"gx": NGX, "gy": NGY}[axis]
    pairs = [(i, i + by) for i in range(count - by) if (i // by) % 2 == which]
    return lax.ppermute(x, axis, pairs + [(j, i) for i, j in pairs])


def per_device(particle_data, particle_cells, slot_counts, fluid_velocity):
    two_0, two_1, zero_a, keys_a = sort_blocks(GROUPS[0], particle_data, particle_cells, slot_counts)
    two_0, two_1 = exchange(two_0, "gx", 2, 0), exchange(two_1, "gx", 2, 1)
    one_0, one_1, zero_b, keys_b = sort_blocks(GROUPS[1], particle_data, particle_cells, slot_counts)
    one_0, one_1 = exchange(one_0, "gx", 1, 0), exchange(one_1, "gx", 1, 1)
    along = [two_0, two_1, jnp.concatenate([zero_a, zero_b], axis=0), one_0, one_1]
    below, mine, above = [jnp.concatenate([a[d * BR:(d + 1) * BR] for a in along], axis=0) for d in range(3)]
    up = lax.rem(lax.axis_index("gy"), 2) == 0
    sides = [
        exchange(jnp.where(up, above, below), "gy", 1, 0),
        exchange(jnp.where(up, below, above), "gy", 1, 1),
    ]
    bases = tuple(range(0, 5 * BR, BR))
    acc = deposit([mine], bases, 8)
    table, own, send_0, send_1, token = deposit(sides, bases, 8, acc, fluid_velocity.reshape(3, 512, 128))
    rows = (own, send_0, send_1, exchange(send_0, "gx", 1, 0), exchange(send_1, "gx", 1, 1))
    *pos, token = inverse(keys_a, keys_b, token)
    packed = pack_edges(rows, token)
    core, beside, moments = sweeps(rows, packed, exchange(packed, "gy", 1, 0), exchange(packed, "gy", 1, 1))
    everyone = lax.all_to_all(moments, ("gx", "gy"), 0, 0)
    pressure, slopes = gradients(everyone, core, beside)
    far_0, far_1, token = interp(sides, bases, table, slopes, 8, token, 2)
    back = [exchange(far_0, "gy", 1, 0), exchange(far_1, "gy", 1, 1)]
    near, _ = interp([mine], bases, table, slopes, 8, token, 1)
    blocks = list(arrange(back[0], near, back[1]))
    for i, (by, which) in ((0, (2, 0)), (1, (2, 1)), (3, (1, 0)), (4, (1, 1))):
        blocks[i] = exchange(blocks[i], "gx", by, which)
    drag = place_forces(blocks, pos)
    return pressure.reshape(64, 8, 128), drag


def solution(mesh):
    return jax.shard_map(
        per_device,
        mesh=mesh,
        in_specs=(
            P(None, ("gx", "gy"), None, None),
            P(None, ("gx", "gy"), None, None),
            P(("gx", "gy"), None),
            P(None, None, "gx", "gy"),
        ),
        out_specs=(P(None, "gx", "gy"), P(None, ("gx", "gy"), None, None)),
        check_vma=False,
    )
```
